32 devices in a mesh: side: 2 (over core), grp: 4 (over y, x), head: 4 (over z).
Axes of the slice: x: 2, y: 2, z: 4, core: 2. Of those that a mesh axis runs over, the one named last changes fastest.
Arguments:
- q_new: bfloat16 [8, 64, 4096], P(('side', 'grp'), None, 'head'), may hold values from -12 to 12
- k_cache: bfloat16 [8, 4, 512, 128], P(('side', 'grp'), 'head'), may hold values from -12 to 12
- value_cache: bfloat16 [8, 4, 512, 128], P(('side', 'grp'), 'head'), may hold values from -12 to 12
- k_new: bfloat16 [8, 64, 512], P(('side', 'grp'), None, 'head'), may hold values from -12 to 12
- new_value_rows: bfloat16 [8, 64, 512], P(('side', 'grp'), None, 'head'), may hold values from -12 to 12
- cache_len: int32 [8], P(('side', 'grp')), may hold values from 1 to 512, 2048 in all
- hidden_in: bfloat16 [8, 64, 2048], P(('side', 'grp'), 'head'), may hold values from -8 to 8
- out_proj: bfloat16 [4096, 2048], P('head', 'side'), may hold values from -0.09375 to 0.09375
- norm_gain: float32 [2048], replicated, may hold values from 0.1 to 1.9
- expert_ids: int32 [8, 64, 8], P(('side', 'grp'), 'head'), may hold values from 0 to 7, all different within a row; in each aligned block of 16 rows (0 to 15, 16 to 31, ..., all dimensions but the last counted through in order) at most 16 rows name the same one
- gate_wts: float32 [8, 64, 8], P(('side', 'grp'), 'head'), may hold values from 0.05 to 1
- w_gate: bfloat16 [8, 2048, 768], P(('side', 'grp'), None, 'head'), may hold values from -0.125 to 0.125
- w_up: bfloat16 [8, 2048, 768], P(('side', 'grp'), None, 'head'), may hold values from -0.125 to 0.125
- w_down: bfloat16 [8, 768, 2048], P(('side', 'grp'), 'head'), may hold values from -0.21875 to 0.21875
Outputs:
- layer_out: bfloat16 [8, 64, 2048], P(('side', 'grp'), 'head')
The draws below stay inside these ranges and needn't reach their ends.
Inputs may be any that keep to these rules, and one draw needn't show every extreme that they name: `expert_ids`: each row names 8 different experts. In each aligned block of 16 rows (one stream's rows taken 16 at a time) no expert is named by more than 16 rows, a bound that some block reaches. `cache_len`: some stream has all 512 positions valid.
All inputs are finite; a program needn't handle non-finite values. No bound on the sum of `cache_len` on one device may be relied on, other than what follows from the above.
Results may differ from the reference program's by a relative error of at most 0.015.
Values may be sent and summed in bfloat16 or wider, within the bound.
A program may use at most 64 MiB of HBM per device.

```python
import math
import jax
import jax.numpy as jnp
import numpy as np
from jax import lax

D = 2048
QUERY_HEADS = 32
KEY_VALUE_HEADS = 4
HEAD_SIZE = 128
FF = 768
TOPK = 8
NEW_TOKEN_ROWS = 64
CACHE_POSITIONS = 512
STREAM_COUNT = 8
EXPERTS = 8
ROWB = 16
FF_PART = 192
MOST = 16
N_HEAD = 4


def attention_parts(key):
    key_q, random_key_cache, random_key_normal = jax.random.split(jax.random.fold_in(key, 7), 3)
    query_rows = jnp.clip(jax.random.normal(key_q, (STREAM_COUNT, NEW_TOKEN_ROWS, QUERY_HEADS * HEAD_SIZE), jnp.float32), -6.0, 6.0)
    cached_part = jnp.clip(jax.random.normal(random_key_cache, (STREAM_COUNT, KEY_VALUE_HEADS, CACHE_POSITIONS, HEAD_SIZE), jnp.float32), -6.0, 6.0)
    fresh_part = jnp.clip(jax.random.normal(random_key_normal, (STREAM_COUNT, NEW_TOKEN_ROWS, KEY_VALUE_HEADS, HEAD_SIZE), jnp.float32), -6.0, 6.0)
    return (query_rows, cached_part, fresh_part.reshape(STREAM_COUNT, NEW_TOKEN_ROWS, KEY_VALUE_HEADS * HEAD_SIZE))


def draw_q_new(key, part):
    return attention_parts(key)[0].astype(jnp.bfloat16)


def draw_k_cache(key, part):
    return attention_parts(key)[1].astype(jnp.bfloat16)


def draw_k_new(key, part):
    return attention_parts(key)[2].astype(jnp.bfloat16)


def draw_hidden_in(key, part):
    key_r, random_key_cache, key_z = jax.random.split(jax.random.fold_in(key, 11), 3)
    row_scale = jnp.exp(jax.random.uniform(key_r, (STREAM_COUNT, NEW_TOKEN_ROWS, 1), jnp.float32, math.log(0.1), 0.0))
    col_scale = jnp.exp(jax.random.uniform(random_key_cache, (D,), jnp.float32, math.log(0.1), 0.0))
    base = jnp.clip(jax.random.normal(key_z, (STREAM_COUNT, NEW_TOKEN_ROWS, D), jnp.float32), -6.0, 6.0)
    return jnp.clip(base * row_scale * col_scale, -8.0, 8.0).astype(jnp.bfloat16)


def shard_levels(own_key, shape, cuts, smallest, top_value):
    factor_of = 1.0
    for position, blocks in cuts:
        draws = jax.random.uniform(jax.random.fold_in(jax.random.fold_in(own_key, 6), position), (blocks,), jnp.float32, smallest / len(cuts), top_value / len(cuts))
        factor_of = factor_of * jnp.repeat(jnp.exp(draws), shape[position] // blocks).reshape((-1,) + (1,) * (len(shape) - 1 - position))
    return factor_of


def length_profile(count, total, reach, lean):
    portions = [(1 << 20) // math.isqrt(standing ** lean) + 1 for standing in range(2, count + 1)]
    spare, counts = total - reach - (count - 1), [1] * (count - 1)
    while spare > 0:
        candidates = [i for i in range(count - 1) if counts[i] < reach]
        mass, budget = sum([portions[i] for i in candidates]), spare
        for i in candidates:
            extra = min(reach - counts[i], max(1, budget * portions[i] // mass), spare)
            counts[i] = counts[i] + extra
            spare = spare - extra
    return np.array([reach] + counts)


def ragged(own_key, amount, total, bound, lean):
    if amount == 2:
        one = jax.random.randint(own_key, (), max(1, total - bound), min(bound, total - 1) + 1)
        return jnp.stack([one, total - one])
    sizes = jnp.asarray(length_profile(amount, total, bound, lean), jnp.int32)
    twos = (amount - 1) // 2
    giver, sink = sizes[1:1 + 2 * twos:2], sizes[2:2 + 2 * twos:2]
    slack = jnp.minimum(giver - 1, bound - sink)
    shifted = jax.random.randint(jax.random.fold_in(own_key, 1), (twos,), 0, 1 << 20) % (slack + 1)
    sizes = sizes.at[1:1 + 2 * twos:2].set(giver - shifted).at[2:2 + 2 * twos:2].set(sink + shifted)
    return sizes[jax.random.permutation(jax.random.fold_in(own_key, 2), amount)]


def shared_out(key, own, number, rows, number_of, top, most, lean):
    ranking = jax.random.permutation(key, number_of)
    packed, common = shares(number_of, rows * top, most, lean, True), shares(number_of, rows * top, most, lean, False)
    places = jnp.arange(number_of)

    def named(tallies, offset_by):
        used = int((tallies > 0).sum())
        fixed = max(1, used // 4)
        shifted = fixed + (places - fixed + offset_by * (used - fixed)) % max(1, number_of - fixed)
        return jnp.zeros((number_of,), jnp.int32).at[ranking[jnp.where(places < fixed, places, shifted)]].set(jnp.asarray(tallies, jnp.int32))

    tallies = jnp.where(number % 4 == 0, named(packed, number // 4), named(common, number - number // 4 - 1))
    mixed = jax.random.permutation(jax.random.fold_in(own, 3), number_of)
    donor, taker = mixed[0:number_of // 2 * 2:2], mixed[1:number_of // 2 * 2:2]
    margin = jnp.minimum(tallies[donor] - 1, most - tallies[taker]) // 2
    margin = jnp.where((donor == ranking[0]) | (taker == ranking[0]) | (tallies[taker] == 0), 0, jnp.maximum(margin, 0))
    shifted = jax.random.randint(jax.random.fold_in(own, 4), (number_of // 2,), 0, 1 << 20) % (margin + 1)
    tallies = tallies.at[donor].add(-shifted).at[taker].add(shifted)
    labels = jnp.searchsorted(jnp.cumsum(tallies), jnp.arange(rows * top), side="right").astype(jnp.int32)
    listing = labels.reshape(top, rows).T
    listing = listing[jax.random.permutation(jax.random.fold_in(own, 1), rows)]
    offset_by = jax.random.randint(jax.random.fold_in(own, 2), (rows, 1), 0, top)
    return jnp.take_along_axis(listing, (jnp.arange(top)[None, :] + offset_by) % top, axis=1)


def shares(number_of, total, bound, lean, full):
    portions = [(1 << 20) // math.isqrt(standing ** lean) + 1 for standing in range(1, number_of + 1)]
    largest = bound if full else min(bound, max(-(-total // number_of), total * portions[0] // sum(portions)))
    least = 1 if total - largest >= number_of - 1 else 0
    holding, surplus = [largest] + [least] * (number_of - 1), total - largest - least * (number_of - 1)
    while surplus > 0:
        candidates = [i for i in range(1, number_of) if holding[i] < largest] or [i for i in range(1, number_of) if holding[i] < bound]
        whole, budget = sum([portions[i] for i in candidates]), surplus
        for i in candidates:
            addition = min(bound - holding[i], max(1, budget * portions[i] // whole), surplus)
            holding[i] = holding[i] + addition
            surplus = surplus - addition
    return np.array(holding)


def centred(stream_key, extent, scale, reach, cuts=(), dtype=jnp.bfloat16):
    entries = jax.random.normal(stream_key, extent, jnp.float32) * scale
    if len(cuts) > 0:
        entries = shard_levels(stream_key, extent, cuts, -0.22, 0.18) * entries
    return jnp.clip(entries, min=-reach, max=reach).astype(dtype)


def setup_inputs(seed: int = 0) -> dict:
    keys = jax.random.split(jax.random.key(seed), 15)
    q_new = draw_q_new(jax.random.fold_in(keys[14], 71), 0)
    k_cache = draw_k_cache(jax.random.fold_in(keys[14], 71), 0)
    value_cache = centred(keys[2], (STREAM_COUNT, KEY_VALUE_HEADS, CACHE_POSITIONS, HEAD_SIZE), 2.0, 12.0, ((0, 8), (1, 4)))
    k_new = draw_k_new(jax.random.fold_in(keys[14], 71), 0)
    new_value_rows = centred(keys[4], (STREAM_COUNT, NEW_TOKEN_ROWS, KEY_VALUE_HEADS * HEAD_SIZE), 2.0, 12.0, ((0, 8), (2, 4)))
    cache_len = ragged(keys[5], STREAM_COUNT, STREAM_COUNT * CACHE_POSITIONS // 2, CACHE_POSITIONS, 2).astype(jnp.int32)
    hidden_in = draw_hidden_in(jax.random.fold_in(keys[14], 71), 0)
    out_proj = centred(keys[7], (QUERY_HEADS * HEAD_SIZE, D), (QUERY_HEADS * HEAD_SIZE) ** -0.5, 0.09375, ((0, 4), (1, 2)))
    norm_gain = jnp.clip(1.0 + 0.18 * jax.random.normal(keys[8], (D,), jnp.float32), 0.1, 1.9)
    expert_ids_keys = jax.random.split(jax.random.fold_in(keys[9], 1), STREAM_COUNT * NEW_TOKEN_ROWS // ROWB)
    expert_ids_turns = jax.random.permutation(jax.random.fold_in(keys[9], 3), STREAM_COUNT * NEW_TOKEN_ROWS // ROWB)
    expert_ids = jax.vmap(lambda own, number: shared_out(jax.random.fold_in(keys[9], 2), own, number, ROWB, EXPERTS, TOPK, MOST, 2))(expert_ids_keys, expert_ids_turns).reshape((STREAM_COUNT, NEW_TOKEN_ROWS, TOPK))
    gate_wts = jnp.clip(jnp.exp(math.log(1.0) - 2.9957323 * jax.random.uniform(keys[10], (STREAM_COUNT, NEW_TOKEN_ROWS, TOPK), jnp.float32) ** shard_levels(keys[10], (STREAM_COUNT, NEW_TOKEN_ROWS, TOPK), ((0, 8), (1, 4)), -0.2, 0.2)), 0.05, 1.0)
    w_gate = centred(keys[11], (EXPERTS, D, FF), D ** -0.5, 0.125, ((0, 8), (2, 4)))
    w_up = centred(keys[12], (EXPERTS, D, FF), D ** -0.5, 0.125, ((0, 8), (2, 4)))
    w_down = centred(keys[13], (EXPERTS, FF, D), FF ** -0.5, 0.21875, ((0, 8), (1, 4)))
    return {"q_new": q_new, "k_cache": k_cache, "value_cache": value_cache, "k_new": k_new, "new_value_rows": new_value_rows, "cache_len": cache_len, "hidden_in": hidden_in, "out_proj": out_proj, "norm_gain": norm_gain, "expert_ids": expert_ids, "gate_wts": gate_wts, "w_gate": w_gate, "w_up": w_up, "w_down": w_down}


def attend_stream(operands):
    query_rows, cached_key_rows, cached_value_rows, fresh_key_rows, fresh_value_rows, valid_len = operands
    query_groups = QUERY_HEADS // KEY_VALUE_HEADS
    joined_keys = jnp.concatenate([cached_key_rows, fresh_key_rows.reshape(NEW_TOKEN_ROWS, KEY_VALUE_HEADS, HEAD_SIZE).transpose(1, 0, 2)], axis=1)
    joined_values = jnp.concatenate([cached_value_rows, fresh_value_rows.reshape(NEW_TOKEN_ROWS, KEY_VALUE_HEADS, HEAD_SIZE).transpose(1, 0, 2)], axis=1)
    reshaped_rows = query_rows.reshape(NEW_TOKEN_ROWS, KEY_VALUE_HEADS, query_groups, HEAD_SIZE)
    scores = jnp.einsum('rjgd,jkd->jgrk', reshaped_rows.astype(jnp.float32), joined_keys.astype(jnp.float32)) / math.sqrt(HEAD_SIZE)
    key_pos = jnp.arange(CACHE_POSITIONS + NEW_TOKEN_ROWS)[None, :]
    row_pos = jnp.arange(NEW_TOKEN_ROWS)[:, None]
    visible = jnp.where(key_pos < CACHE_POSITIONS, key_pos < valid_len, key_pos - CACHE_POSITIONS <= row_pos)
    scores = jnp.where(visible, scores, -jnp.inf)
    highest = lax.optimization_barrier(jnp.max(scores, axis=-1, keepdims=True))
    exp_scores = jnp.exp(scores - highest)
    attn_probs = (exp_scores / lax.optimization_barrier(jnp.sum(exp_scores, axis=-1, keepdims=True))).astype(jnp.bfloat16)
    context = jnp.einsum('jgrk,jkd->rjgd', attn_probs.astype(jnp.float32), joined_values.astype(jnp.float32)).astype(jnp.bfloat16)
    return context.reshape(NEW_TOKEN_ROWS, QUERY_HEADS * HEAD_SIZE)

def reference(q_new, k_cache, value_cache, k_new, new_value_rows, cache_len, hidden_in, out_proj, norm_gain, expert_ids, gate_wts, w_gate, w_up, w_down):
    context = lax.map(attend_stream, (q_new, k_cache, value_cache, k_new, new_value_rows, cache_len))
    total_rows = STREAM_COUNT * NEW_TOKEN_ROWS
    attn_out = jnp.dot(context.reshape(total_rows, QUERY_HEADS * HEAD_SIZE), out_proj, preferred_element_type=jnp.float32)
    resid = hidden_in.reshape(total_rows, D).astype(jnp.float32) + attn_out
    normed = (resid * lax.rsqrt(lax.optimization_barrier(jnp.mean(resid * resid, axis=-1, keepdims=True)) + 1e-06) * norm_gain).astype(jnp.bfloat16)
    raw_wts = gate_wts.reshape(total_rows, TOPK)
    mixing = (raw_wts / lax.optimization_barrier(jnp.sum(raw_wts, axis=-1, keepdims=True))).astype(jnp.bfloat16)
    chosen = expert_ids.reshape(total_rows, TOPK).astype(jnp.int32)
    blocks = total_rows // ROWB
    by_block = chosen.reshape(blocks, ROWB * TOPK)
    one_hot = (by_block[:, :, None] == jnp.arange(EXPERTS).astype(jnp.int32)[None, None, :]).astype(jnp.int32)
    earlier = jnp.cumsum(one_hot, axis=1) - one_hot
    slot_index = lax.optimization_barrier(jnp.sum(earlier * one_hot, axis=-1))
    column = (jnp.arange(blocks).astype(jnp.int32)[:, None] * MOST + slot_index).reshape(-1).astype(jnp.int32)
    row_index = jnp.repeat(jnp.arange(total_rows).astype(jnp.int32), TOPK)
    expert_flat = chosen.reshape(-1)
    table = jnp.full((EXPERTS, blocks * MOST), total_rows, jnp.int32).at[expert_flat, column].set(row_index)
    wtable = jnp.zeros((EXPERTS, blocks * MOST), jnp.float32).at[expert_flat, column].set(mixing.reshape(-1).astype(jnp.float32))
    padded = jnp.concatenate([normed, jnp.zeros((1, D), jnp.bfloat16)], axis=0)

    def expert_step(running, operands):
        slot_rows, slot_wts, gate_mat, up_mat, down_mat = operands
        gathered = padded[slot_rows]
        gate_proj = jnp.dot(gathered, gate_mat, preferred_element_type=jnp.float32)
        up_proj = jnp.dot(gathered, up_mat, preferred_element_type=jnp.float32)
        hidden = (jax.nn.silu(gate_proj) * up_proj).astype(jnp.bfloat16)
        partial_value = jnp.einsum('nqf,qfd->nqd', hidden.reshape(-1, N_HEAD, FF_PART).astype(jnp.float32), down_mat.reshape(N_HEAD, FF_PART, D).astype(jnp.float32)).astype(jnp.bfloat16)
        addend = slot_wts[:, None] * lax.optimization_barrier(jnp.sum(partial_value.astype(jnp.float32), axis=1))
        return (running.at[slot_rows].add(addend), None)
    running = jnp.zeros((total_rows + 1, D), jnp.float32)
    running = lax.scan(expert_step, running, (table, wtable, w_gate, w_up, w_down))[0]
    layer_out = (resid + running[:total_rows]).astype(jnp.bfloat16)
    return layer_out.reshape(STREAM_COUNT, NEW_TOKEN_ROWS, D)
```

```python
import math

import jax
import jax.numpy as jnp
from jax import lax
from jax.experimental import pallas as pl
from jax.experimental.pallas import tpu as pltpu
from jax.sharding import PartitionSpec as P

LANES = 128
CHUNK = 256
MESH = pl.DeviceIdType.MESH
NT = (((1,), (1,)), ((), ()))


def attend(q_new, k_cache, value_cache, k_new, new_value_rows, cache_len):
    q_rows = q_new.shape[1]
    head_dim = k_cache.shape[3]
    cached_part = k_cache.shape[2]
    query_groups = q_new.shape[2] // head_dim
    joined_keys = jnp.concatenate([k_cache[0, 0], k_new[0]], axis=0)
    joined_values = jnp.concatenate([value_cache[0, 0], new_value_rows[0]], axis=0)
    query_rows = q_new[0].reshape(q_rows, query_groups, head_dim)
    scores = jnp.einsum(
        "rgd,kd->grk", query_rows, joined_keys, preferred_element_type=jnp.float32
    ) / math.sqrt(head_dim)
    key_pos = jnp.arange(cached_part + q_rows)[None, :]
    row_pos = jnp.arange(q_rows)[:, None]
    visible = jnp.where(
        key_pos < cached_part, key_pos < cache_len[0], key_pos - cached_part <= row_pos
    )
    scores = jnp.where(visible[None], scores, -jnp.inf)
    highest = jnp.max(scores, axis=-1, keepdims=True)
    exp_scores = jnp.exp(scores - highest)
    attn_probs = (exp_scores / jnp.sum(exp_scores, axis=-1, keepdims=True)).astype(jnp.bfloat16)
    context = jnp.einsum(
        "grk,kd->rgd", attn_probs, joined_values, preferred_element_type=jnp.float32
    ).astype(jnp.bfloat16)
    return context.reshape(q_rows, query_groups * head_dim)


def routing_tables(chosen, mixing, experts, most):
    rows_here, top_k = chosen.shape
    one_hot = (
        (chosen[:, :, None] == jnp.arange(experts)[None, None, :])
        .astype(jnp.int32)
        .reshape(rows_here * top_k, experts)
    )
    earlier = jnp.cumsum(one_hot, axis=0) - one_hot
    slot_index = jnp.sum(earlier * one_hot, axis=1)
    target = chosen.reshape(-1) * most + slot_index
    matches = (jnp.arange(experts * most)[:, None] == target[None, :]).reshape(
        experts * most, rows_here, top_k
    )
    dispatch = jnp.any(matches, axis=2).astype(jnp.bfloat16)
    combine = jnp.sum(jnp.where(matches, mixing.astype(jnp.float32)[None], 0.0), axis=2).T.astype(
        jnp.bfloat16
    )
    return (dispatch, combine)


def shards_sparse(
    q_new,
    k_cache,
    value_cache,
    k_new,
    new_value_rows,
    cache_len,
    hidden_in,
    out_proj,
    norm_gain,
    expert_ids,
    gate_wts,
    w_gate,
    w_up,
    w_down,
):
    context = attend(q_new, k_cache, value_cache, k_new, new_value_rows, cache_len)
    width = hidden_in.shape[2]
    halves = jnp.einsum(
        "sre,ec->src",
        lax.all_gather(context[None], "side", axis=0, tiled=True),
        out_proj,
        preferred_element_type=jnp.float32,
    )
    summed = lax.psum_scatter(
        halves.astype(jnp.bfloat16), "head", scatter_dimension=1, tiled=True
    ).astype(jnp.float32)
    attn_out = lax.all_to_all(
        summed.astype(jnp.bfloat16), "side", split_axis=0, concat_axis=2, tiled=True
    ).astype(summed.dtype)[0]
    resid = hidden_in[0].astype(jnp.float32) + attn_out
    normed = (
        resid * lax.rsqrt(jnp.mean(resid * resid, axis=-1, keepdims=True) + 1e-06) * norm_gain
    ).astype(jnp.bfloat16)
    raw_wts = gate_wts[0]
    mixing = (raw_wts / jnp.sum(raw_wts, axis=-1, keepdims=True)).astype(jnp.bfloat16)
    experts = lax.axis_size("side") * lax.axis_size("grp")
    quarters = lax.axis_size("head")
    rows_here = expert_ids.shape[1]
    top_k = expert_ids.shape[2]
    most = max(2, (rows_here * top_k + experts - 1) // experts)
    dispatch, combine = routing_tables(expert_ids[0], mixing, experts, most)
    group_rows, group_dispatch = (
        lax.all_gather(normed[None], "head", axis=0, tiled=True),
        lax.all_gather(dispatch[None], "head", axis=0, tiled=True),
    )
    outgoing = (
        jnp.einsum("hsr,hrd->hsd", group_dispatch, group_rows, preferred_element_type=jnp.float32)
        .astype(jnp.bfloat16)
        .reshape(quarters, experts, most, width)
    )
    slot_rows = lax.all_to_all(outgoing, ("side", "grp"), split_axis=1, concat_axis=1, tiled=True)
    flat_rows = slot_rows.reshape(-1, width)
    gate_proj = jnp.dot(flat_rows, w_gate[0], preferred_element_type=jnp.float32)
    up_proj = jnp.dot(flat_rows, w_up[0], preferred_element_type=jnp.float32)
    hidden = (jax.nn.silu(gate_proj) * up_proj).astype(jnp.bfloat16)
    partial_value = (
        jnp.dot(hidden, w_down[0], preferred_element_type=jnp.float32)
        .astype(jnp.bfloat16)
        .reshape(quarters, experts, most, width)
    )
    combine_all = lax.all_gather(combine[None], "head", axis=0, tiled=True)
    returned = lax.all_to_all(
        partial_value, ("side", "grp"), split_axis=1, concat_axis=1, tiled=True
    )
    weighted = jnp.einsum(
        "hrs,hsd->hrd",
        combine_all,
        returned.reshape(quarters, experts * most, width),
        preferred_element_type=jnp.float32,
    )
    moe_out = lax.psum_scatter(
        weighted.astype(jnp.bfloat16), "head", scatter_dimension=0, tiled=True
    ).astype(jnp.float32)[0]
    return (resid + moe_out).astype(jnp.bfloat16)[None]


def dense_kernel(
    q_hbm, kc_hbm, vc_hbm, kn_hbm, vn_hbm, len_ref, hid_hbm, wo_hbm, gain_hbm, ids_hbm, wts_hbm,
    wg_hbm, wu_hbm, wd_hbm,
    out_ref,
    q, kc, vc, kn, vn, hid, wo, gain, ids, wts, wg, wu, wd,
    ctx, part, part_in, resid, rows, y, y_sib, y_sum, y_in, z, z_in,
    load_sem, ctx_send, ctx_recv, part_send, part_recv, z_send, z_recv, sib_send, sib_recv,
    xy_send, xy_recv, fwd_send, fwd_recv, ys_send, ys_recv, yx_send, yx_recv, zo_send, zo_recv,
):
    side, grp, head = lax.axis_index("side"), lax.axis_index("grp"), lax.axis_index("head")
    sides, heads = ctx.shape[0], rows.shape[2]
    groups, rows_here, width = y.shape[0], y.shape[3], y.shape[4]
    other = 1 - side

    def group(k):
        return lax.rem(grp // 2 + k // 2, 2) * 2 + lax.rem(lax.rem(grp, 2) + k % 2, 2)

    def ahead(step):
        return lax.rem(head + step, heads)

    def behind(step):
        return lax.rem(head + heads - step, heads)

    loads = [
        pltpu.make_async_copy(src, dst, load_sem.at[i])
        for i, (src, dst) in enumerate(
            [
                (q_hbm.at[0], q), (kc_hbm.at[0, 0], kc), (kn_hbm.at[0], kn),
                (vc_hbm.at[0, 0], vc), (vn_hbm.at[0], vn), (wo_hbm, wo), (hid_hbm.at[0], hid),
                (gain_hbm, gain), (ids_hbm.at[0], ids), (wts_hbm.at[0], wts),
                (wg_hbm.at[0], wg), (wu_hbm.at[0], wu), (wd_hbm.at[0], wd),
            ]
        )
    ]
    for load in loads:
        load.start()

    barrier = pltpu.get_barrier_semaphore()
    peers = [(other, grp, head)]
    for step in range(1, heads):
        peers += [(side, grp, ahead(step)), (other, grp, ahead(step))]
    peers += [(side, group(k), head) for k in range(1, groups)]
    for peer in peers:
        pl.semaphore_signal(barrier, inc=1, device_id=peer, device_id_type=MESH)

    started = []

    def send(src, dst, send_sem, recv_sem, peer):
        copy = pltpu.make_async_remote_copy(
            src_ref=src, dst_ref=dst, send_sem=send_sem, recv_sem=recv_sem,
            device_id=peer, device_id_type=MESH,
        )
        copy.start()
        started.append(copy)
        return copy

    new_rows, head_dim = kn.shape
    cached = kc.shape[0]
    per_chunk = CHUNK // head_dim
    chunks = q.shape[1] // CHUNK
    scale = 1.0 / math.sqrt(head_dim)
    for load in loads[:5]:
        load.wait()
    valid = len_ref[0]
    chunk_rows = per_chunk * new_rows
    seen_cached = lax.broadcasted_iota(jnp.int32, (chunk_rows, cached), 1) < valid
    row_pos = lax.rem(lax.broadcasted_iota(jnp.int32, (chunk_rows, new_rows), 0), new_rows)
    seen_new = lax.broadcasted_iota(jnp.int32, (chunk_rows, new_rows), 1) <= row_pos
    ctx_copies = []
    for c in range(chunks):
        queries = jnp.concatenate(
            [q[:, c * CHUNK + j * head_dim : c * CHUNK + (j + 1) * head_dim] for j in range(per_chunk)],
            axis=0,
        )
        s_old = lax.dot_general(queries, kc[...], NT, preferred_element_type=jnp.float32) * scale
        s_new = lax.dot_general(queries, kn[...], NT, preferred_element_type=jnp.float32) * scale
        s_old = jnp.where(seen_cached, s_old, -jnp.inf)
        s_new = jnp.where(seen_new, s_new, -jnp.inf)
        highest = jnp.maximum(
            jnp.max(s_old, axis=1, keepdims=True), jnp.max(s_new, axis=1, keepdims=True)
        )
        e_old, e_new = jnp.exp(s_old - highest), jnp.exp(s_new - highest)
        inverse = 1.0 / (
            jnp.sum(e_old, axis=1, keepdims=True) + jnp.sum(e_new, axis=1, keepdims=True)
        )
        p_old = (e_old * inverse).astype(jnp.bfloat16)
        p_new = (e_new * inverse).astype(jnp.bfloat16)
        found = jnp.dot(p_old, vc[...], preferred_element_type=jnp.float32) + jnp.dot(
            p_new, vn[...], preferred_element_type=jnp.float32
        )
        found = found.astype(jnp.bfloat16)
        for j in range(per_chunk):
            ctx[side, c, :, j * head_dim : (j + 1) * head_dim] = found[
                j * new_rows : (j + 1) * new_rows
            ]
        if c == 0:
            pl.semaphore_wait(barrier, len(peers))
        ctx_copies.append(
            send(
                ctx.at[side, c], ctx.at[side, c], ctx_send.at[c], ctx_recv.at[c],
                (other, grp, head),
            )
        )

    for load in loads[5:10]:
        load.wait()
    raw = wts[...]
    mixing = (raw / jnp.sum(raw, axis=0, keepdims=True)).astype(jnp.bfloat16).astype(jnp.float32)
    expert = lax.broadcasted_iota(jnp.int32, (LANES, rows_here), 0)
    table = jnp.zeros((LANES, rows_here), jnp.float32)
    for k in range(raw.shape[0]):
        table += jnp.where(ids[k : k + 1, :] == expert, mixing[k : k + 1, :], 0.0)
    unit = (
        lax.broadcasted_iota(jnp.int32, (rows_here, rows_here), 0)
        == lax.broadcasted_iota(jnp.int32, (rows_here, rows_here), 1)
    )
    unit = jnp.where(unit, 1.0, 0.0).astype(jnp.bfloat16)
    table = lax.dot_general(
        unit, table.astype(jnp.bfloat16), NT, preferred_element_type=jnp.float32
    )
    rows[grp, side, head, :, width:] = table.astype(jnp.bfloat16)

    for copy in ctx_copies:
        copy.wait_recv()
    half = wo.shape[1]
    for n in range(0, half, CHUNK):
        total = jnp.zeros((sides * new_rows, CHUNK), jnp.float32)
        for c in range(chunks):
            total += jnp.dot(
                ctx[:, c].reshape(sides * new_rows, CHUNK),
                wo[c * CHUNK : (c + 1) * CHUNK, n : n + CHUNK],
                preferred_element_type=jnp.float32,
            )
        part[:, :, :, n : n + CHUNK] = total.astype(jnp.bfloat16).reshape(
            sides, heads, rows_here, CHUNK
        )
    part_copies = []
    for step in range(heads - 1, -1, -1):
        for turn in range(sides):
            if step == 0 and turn == 0:
                continue
            to_side = side if turn == 0 else other
            slot = turn * heads + step
            part_copies.append(
                send(
                    part.at[to_side, ahead(step)], part_in.at[side, head],
                    part_send.at[slot], part_recv.at[slot], (to_side, grp, ahead(step)),
                )
            )
    part_in[side, head] = part[side, head]
    for copy in part_copies:
        copy.wait_recv()
    square = jnp.zeros((rows_here, 1), jnp.float32)
    for piece in range(sides):
        columns = slice(piece * half, (piece + 1) * half)
        value = hid[:, columns].astype(jnp.float32)
        for j in range(heads):
            value += part_in[piece, j].astype(jnp.float32)
        resid[:, columns] = value
        square += jnp.sum(value * value, axis=1, keepdims=True)
    inv_norm = lax.rsqrt(square * (1.0 / width) + 1e-06)
    rows[grp, side, head, :, :width] = (resid[...] * inv_norm * gain[...]).astype(jnp.bfloat16)

    block = rows.at[grp, side, head]
    z_copies = [None]
    for step in range(1, heads):
        z_copies.append(
            send(block, block, z_send.at[step], z_recv.at[step], (side, grp, ahead(step)))
        )
    sib_copies, xy_copies = [], [[] for _ in range(groups)]

    def spread(step):
        piece = rows.at[grp, side, behind(step)]
        for k in range(1, groups):
            xy_copies[k].append(
                send(
                    piece, piece, xy_send.at[k, step], xy_recv.at[k, step],
                    (side, group(k), head),
                )
            )
        sib_copies.append(
            send(piece, piece, sib_send.at[step], sib_recv.at[step], (other, grp, head))
        )

    spread(0)
    for step in range(1, heads):
        z_copies[step].wait_recv()
        spread(step)

    fwd_copies, ys_copies, yx_copies = [None] * groups, [None] * groups, [None] * groups

    def forward(k):
        for copy in xy_copies[k]:
            copy.wait_recv()
        pieces = rows.at[group(k), side]
        fwd_copies[k] = send(pieces, pieces, fwd_send.at[k], fwd_recv.at[k], (other, grp, head))

    own_expert = side * groups + grp
    many = sides * heads * rows_here

    def experts(k):
        at = group(k)
        x = rows[at, :, :, :, :width].reshape(many, width)
        gate = lax.dot_general(x, wg[...], NT, preferred_element_type=jnp.float32)
        up = lax.dot_general(x, wu[...], NT, preferred_element_type=jnp.float32)
        hidden = (gate / (1.0 + jnp.exp(-gate)) * up).astype(jnp.bfloat16)
        weights = rows[at, :, :, :, width:].reshape(many, LANES).astype(jnp.float32)
        lane = lax.broadcasted_iota(jnp.int32, (many, LANES), 1)
        column = jnp.sum(jnp.where(lane == own_expert, weights, 0.0), axis=1, keepdims=True)
        for n in range(0, width, 2 * CHUNK):
            value = jnp.dot(hidden, wd[:, n : n + 2 * CHUNK], preferred_element_type=jnp.float32)
            value = value.astype(jnp.bfloat16).astype(jnp.float32) * column
            y[at, :, :, :, n : n + 2 * CHUNK] = value.astype(jnp.bfloat16).reshape(
                sides, heads, rows_here, 2 * CHUNK
            )
        ys_copies[k] = send(
            y.at[at, other], y_sib.at[k], ys_send.at[k], ys_recv.at[k], (other, grp, head)
        )

    def reduce_pair(k):
        ys_copies[k].wait_recv()
        value = y[group(k), side].astype(jnp.float32) + y_sib[k].astype(jnp.float32)
        y_sum[k] = value.astype(jnp.bfloat16)
        yx_copies[k] = send(
            y_sum.at[k], y_in.at[k], yx_send.at[k], yx_recv.at[k], (side, group(k), head)
        )

    forward(1)
    for copy in sib_copies:
        copy.wait_recv()
    for load in loads[10:]:
        load.wait()
    experts(0)
    forward(2)
    fwd_copies[1].wait_recv()
    experts(1)
    forward(3)
    fwd_copies[2].wait_recv()
    experts(2)
    reduce_pair(1)
    fwd_copies[3].wait_recv()
    experts(3)
    reduce_pair(2)
    reduce_pair(3)
    ys_copies[0].wait_recv()
    for k in range(1, groups):
        yx_copies[k].wait_recv()
    for j in range(heads):
        value = y[grp, side, j].astype(jnp.float32) + y_sib[0, j].astype(jnp.float32)
        for k in range(1, groups):
            value += y_in[k, j].astype(jnp.float32)
        z[j] = value.astype(jnp.bfloat16)
    zo_copies = []
    for step in range(heads - 1, 0, -1):
        zo_copies.append(
            send(
                z.at[ahead(step)], z_in.at[step], zo_send.at[step], zo_recv.at[step],
                (side, grp, ahead(step)),
            )
        )
    value = resid[...] + z[head].astype(jnp.float32)
    for copy in zo_copies:
        copy.wait_recv()
    for step in range(1, heads):
        value += z_in[step].astype(jnp.float32)
    out_ref[0] = value.astype(jnp.bfloat16)
    for copy in started:
        copy.wait_send()


def dense_fits(args):
    q_new, hidden_in, expert_ids, w_down = args[0], args[6], args[9], args[13]
    sides, groups, heads = (lax.axis_size(name) for name in ("side", "grp", "head"))
    rows_here, top_k = expert_ids.shape[1:]
    return (
        2 * top_k >= sides * groups
        and sides == 2
        and groups == 4
        and sides * groups <= LANES
        and rows_here % 16 == 0
        and q_new.shape[1] == heads * rows_here
        and q_new.shape[2] % CHUNK == 0
        and hidden_in.shape[2] % (2 * CHUNK) == 0
    )


def shards_dense(
    q_new, k_cache, value_cache, k_new, new_value_rows, cache_len, hidden_in, out_proj, norm_gain,
    expert_ids, gate_wts, w_gate, w_up, w_down,
):
    sides, groups, heads = (lax.axis_size(name) for name in ("side", "grp", "head"))
    new_rows = q_new.shape[1]
    rows_here, width = hidden_in.shape[1:]
    half = out_proj.shape[1]
    chunks = q_new.shape[2] // CHUNK
    operands = (
        q_new, k_cache, value_cache, k_new, new_value_rows, cache_len, hidden_in, out_proj,
        norm_gain.reshape(1, width),
        jnp.swapaxes(expert_ids, 1, 2), jnp.swapaxes(gate_wts, 1, 2),
        jnp.swapaxes(w_gate, 1, 2), jnp.swapaxes(w_up, 1, 2), w_down,
    )
    specs = [pl.BlockSpec(memory_space=pltpu.HBM)] * len(operands)
    specs[5] = pl.BlockSpec(memory_space=pltpu.SMEM)
    bf16 = jnp.bfloat16
    landed = [
        pltpu.VMEM(operands[i].shape[cut:], operands[i].dtype)
        for i, cut in (
            (0, 1), (1, 2), (2, 2), (3, 1), (4, 1), (6, 1), (7, 0), (8, 0), (9, 1), (10, 1),
            (11, 1), (12, 1), (13, 1),
        )
    ]
    dma = pltpu.SemaphoreType.DMA
    return pl.pallas_call(
        dense_kernel,
        out_shape=jax.ShapeDtypeStruct(hidden_in.shape, bf16),
        in_specs=specs,
        out_specs=pl.BlockSpec(memory_space=pltpu.VMEM),
        scratch_shapes=landed
        + [
            pltpu.VMEM((sides, chunks, new_rows, CHUNK), bf16),
            pltpu.VMEM((sides, heads, rows_here, half), bf16),
            pltpu.VMEM((sides, heads, rows_here, half), bf16),
            pltpu.VMEM((rows_here, width), jnp.float32),
            pltpu.VMEM((groups, sides, heads, rows_here, width + LANES), bf16),
            pltpu.VMEM((groups, sides, heads, rows_here, width), bf16),
            pltpu.VMEM((groups, heads, rows_here, width), bf16),
            pltpu.VMEM((groups, heads, rows_here, width), bf16),
            pltpu.VMEM((groups, heads, rows_here, width), bf16),
            pltpu.VMEM((heads, rows_here, width), bf16),
            pltpu.VMEM((heads, rows_here, width), bf16),
            dma((len(landed),)),
            dma((chunks,)), dma((chunks,)),
            dma((sides * heads,)), dma((sides * heads,)),
            dma((heads,)), dma((heads,)),
            dma((heads,)), dma((heads,)),
            dma((groups, heads)), dma((groups, heads)),
            dma((groups,)), dma((groups,)),
            dma((groups,)), dma((groups,)),
            dma((groups,)), dma((groups,)),
            dma((heads,)), dma((heads,)),
        ],
        compiler_params=pltpu.CompilerParams(
            collective_id=0, has_side_effects=True, vmem_limit_bytes=48 * 1024 * 1024
        ),
    )(*operands)


def solution(mesh):
    in_specs = (
        P(("side", "grp"), None, "head"),
        P(("side", "grp"), "head", None, None),
        P(("side", "grp"), "head", None, None),
        P(("side", "grp"), None, "head"),
        P(("side", "grp"), None, "head"),
        P(("side", "grp")),
        P(("side", "grp"), "head", None),
        P("head", "side"),
        P(),
        P(("side", "grp"), "head", None),
        P(("side", "grp"), "head", None),
        P(("side", "grp"), None, "head"),
        P(("side", "grp"), None, "head"),
        P(("side", "grp"), "head", None),
    )
    out_specs = P(("side", "grp"), "head", None)
    def shards(*args):
        if dense_fits(args):
            return shards_dense(*args)
        return shards_sparse(*args)

    return jax.shard_map(shards, mesh=mesh, in_specs=in_specs, out_specs=out_specs, check_vma=False)
```

```python
import math

import jax
import jax.numpy as jnp
from jax import lax
from jax.experimental import pallas as pl
from jax.experimental.pallas import tpu as pltpu
from jax.sharding import PartitionSpec as P

LANES = 128
CHUNK = 256
MESH = pl.DeviceIdType.MESH
NT = (((1,), (1,)), ((), ()))


def attend(q_new, k_cache, value_cache, k_new, new_value_rows, cache_len):
    q_rows = q_new.shape[1]
    head_dim = k_cache.shape[3]
    cached_part = k_cache.shape[2]
    query_groups = q_new.shape[2] // head_dim
    joined_keys = jnp.concatenate([k_cache[0, 0], k_new[0]], axis=0)
    joined_values = jnp.concatenate([value_cache[0, 0], new_value_rows[0]], axis=0)
    query_rows = q_new[0].reshape(q_rows, query_groups, head_dim)
    scores = jnp.einsum(
        "rgd,kd->grk", query_rows, joined_keys, preferred_element_type=jnp.float32
    ) / math.sqrt(head_dim)
    key_pos = jnp.arange(cached_part + q_rows)[None, :]
    row_pos = jnp.arange(q_rows)[:, None]
    visible = jnp.where(
        key_pos < cached_part, key_pos < cache_len[0], key_pos - cached_part <= row_pos
    )
    scores = jnp.where(visible[None], scores, -jnp.inf)
    highest = jnp.max(scores, axis=-1, keepdims=True)
    exp_scores = jnp.exp(scores - highest)
    attn_probs = (exp_scores / jnp.sum(exp_scores, axis=-1, keepdims=True)).astype(jnp.bfloat16)
    context = jnp.einsum(
        "grk,kd->rgd", attn_probs, joined_values, preferred_element_type=jnp.float32
    ).astype(jnp.bfloat16)
    return context.reshape(q_rows, query_groups * head_dim)


def routing_tables(chosen, mixing, experts, most):
    rows_here, top_k = chosen.shape
    one_hot = (
        (chosen[:, :, None] == jnp.arange(experts)[None, None, :])
        .astype(jnp.int32)
        .reshape(rows_here * top_k, experts)
    )
    earlier = jnp.cumsum(one_hot, axis=0) - one_hot
    slot_index = jnp.sum(earlier * one_hot, axis=1)
    target = chosen.reshape(-1) * most + slot_index
    matches = (jnp.arange(experts * most)[:, None] == target[None, :]).reshape(
        experts * most, rows_here, top_k
    )
    dispatch = jnp.any(matches, axis=2).astype(jnp.bfloat16)
    combine = jnp.sum(jnp.where(matches, mixing.astype(jnp.float32)[None], 0.0), axis=2).T.astype(
        jnp.bfloat16
    )
    return (dispatch, combine)


def shards_sparse(
    q_new,
    k_cache,
    value_cache,
    k_new,
    new_value_rows,
    cache_len,
    hidden_in,
    out_proj,
    norm_gain,
    expert_ids,
    gate_wts,
    w_gate,
    w_up,
    w_down,
):
    context = attend(q_new, k_cache, value_cache, k_new, new_value_rows, cache_len)
    width = hidden_in.shape[2]
    halves = jnp.einsum(
        "sre,ec->src",
        lax.all_gather(context[None], "side", axis=0, tiled=True),
        out_proj,
        preferred_element_type=jnp.float32,
    )
    summed = lax.psum_scatter(
        halves.astype(jnp.bfloat16), "head", scatter_dimension=1, tiled=True
    ).astype(jnp.float32)
    attn_out = lax.all_to_all(
        summed.astype(jnp.bfloat16), "side", split_axis=0, concat_axis=2, tiled=True
    ).astype(summed.dtype)[0]
    resid = hidden_in[0].astype(jnp.float32) + attn_out
    normed = (
        resid * lax.rsqrt(jnp.mean(resid * resid, axis=-1, keepdims=True) + 1e-06) * norm_gain
    ).astype(jnp.bfloat16)
    raw_wts = gate_wts[0]
    mixing = (raw_wts / jnp.sum(raw_wts, axis=-1, keepdims=True)).astype(jnp.bfloat16)
    experts = lax.axis_size("side") * lax.axis_size("grp")
    quarters = lax.axis_size("head")
    rows_here = expert_ids.shape[1]
    top_k = expert_ids.shape[2]
    most = max(2, (rows_here * top_k + experts - 1) // experts)
    dispatch, combine = routing_tables(expert_ids[0], mixing, experts, most)
    group_rows, group_dispatch = (
        lax.all_gather(normed[None], "head", axis=0, tiled=True),
        lax.all_gather(dispatch[None], "head", axis=0, tiled=True),
    )
    outgoing = (
        jnp.einsum("hsr,hrd->hsd", group_dispatch, group_rows, preferred_element_type=jnp.float32)
        .astype(jnp.bfloat16)
        .reshape(quarters, experts, most, width)
    )
    slot_rows = lax.all_to_all(outgoing, ("side", "grp"), split_axis=1, concat_axis=1, tiled=True)
    flat_rows = slot_rows.reshape(-1, width)
    gate_proj = jnp.dot(flat_rows, w_gate[0], preferred_element_type=jnp.float32)
    up_proj = jnp.dot(flat_rows, w_up[0], preferred_element_type=jnp.float32)
    hidden = (jax.nn.silu(gate_proj) * up_proj).astype(jnp.bfloat16)
    partial_value = (
        jnp.dot(hidden, w_down[0], preferred_element_type=jnp.float32)
        .astype(jnp.bfloat16)
        .reshape(quarters, experts, most, width)
    )
    combine_all = lax.all_gather(combine[None], "head", axis=0, tiled=True)
    returned = lax.all_to_all(
        partial_value, ("side", "grp"), split_axis=1, concat_axis=1, tiled=True
    )
    weighted = jnp.einsum(
        "hrs,hsd->hrd",
        combine_all,
        returned.reshape(quarters, experts * most, width),
        preferred_element_type=jnp.float32,
    )
    moe_out = lax.psum_scatter(
        weighted.astype(jnp.bfloat16), "head", scatter_dimension=0, tiled=True
    ).astype(jnp.float32)[0]
    return (resid + moe_out).astype(jnp.bfloat16)[None]


def dense_kernel(
    q_hbm, kc_hbm, vc_hbm, kn_hbm, vn_hbm, len_ref, hid_hbm, wo_hbm, gain_hbm, ids_hbm, wts_hbm,
    wg_hbm, wu_hbm, wd_hbm,
    out_ref,
    q, kc, vc, kn, vn, hid, wo, gain, ids, wts, wg, wu, wd,
    ctx, part, part_in, resid, rows, y, y_sib, y_sum, y_a, y_fwd, y_b, z, z_in,
    load_sem, ctx_send, ctx_recv, part_send, part_recv, z_send, z_recv, sib_send, sib_recv,
    xy_send, xy_recv, ys_send, ys_recv, ya_send, ya_recv, yb_send, yb_recv, zo_send, zo_recv,
):
    side, grp, head = lax.axis_index("side"), lax.axis_index("grp"), lax.axis_index("head")
    heads, sides, groups, rows_here, width = y.shape
    other = 1 - side

    def group(k):
        return lax.rem(grp // 2 + k // 2, 2) * 2 + lax.rem(lax.rem(grp, 2) + k % 2, 2)

    def ahead(step):
        return lax.rem(head + step, heads)

    def behind(step):
        return lax.rem(head + heads - step, heads)

    loads = [
        pltpu.make_async_copy(src, dst, load_sem.at[i])
        for i, (src, dst) in enumerate(
            [
                (q_hbm.at[0], q), (kc_hbm.at[0, 0], kc), (kn_hbm.at[0], kn),
                (vc_hbm.at[0, 0], vc), (vn_hbm.at[0], vn), (wo_hbm, wo), (hid_hbm.at[0], hid),
                (gain_hbm, gain), (ids_hbm.at[0], ids), (wts_hbm.at[0], wts),
                (wg_hbm.at[0], wg), (wu_hbm.at[0], wu), (wd_hbm.at[0], wd),
            ]
        )
    ]
    for load in loads:
        load.start()

    barrier = pltpu.get_barrier_semaphore()
    peers = [(other, grp, head)]
    for step in range(1, heads):
        peers += [(side, grp, ahead(step)), (other, grp, ahead(step))]
    peers += [(side, group(1), head), (side, group(2), head)]
    for peer in peers:
        pl.semaphore_signal(barrier, inc=1, device_id=peer, device_id_type=MESH)

    started = []

    def send(src, dst, send_sem, recv_sem, peer):
        copy = pltpu.make_async_remote_copy(
            src_ref=src, dst_ref=dst, send_sem=send_sem, recv_sem=recv_sem,
            device_id=peer, device_id_type=MESH,
        )
        copy.start()
        started.append(copy)
        return copy

    new_rows, head_dim = kn.shape
    cached = kc.shape[0]
    per_chunk = CHUNK // head_dim
    chunks = q.shape[1] // CHUNK
    scale = 1.0 / math.sqrt(head_dim)
    for load in loads[:5]:
        load.wait()
    valid = len_ref[0]
    chunk_rows = per_chunk * new_rows
    seen_cached = lax.broadcasted_iota(jnp.int32, (chunk_rows, cached), 1) < valid
    row_pos = lax.rem(lax.broadcasted_iota(jnp.int32, (chunk_rows, new_rows), 0), new_rows)
    seen_new = lax.broadcasted_iota(jnp.int32, (chunk_rows, new_rows), 1) <= row_pos
    ctx_copies = []
    for c in range(chunks):
        queries = jnp.concatenate(
            [q[:, c * CHUNK + j * head_dim : c * CHUNK + (j + 1) * head_dim] for j in range(per_chunk)],
            axis=0,
        )
        s_old = lax.dot_general(queries, kc[...], NT, preferred_element_type=jnp.float32) * scale
        s_new = lax.dot_general(queries, kn[...], NT, preferred_element_type=jnp.float32) * scale
        s_old = jnp.where(seen_cached, s_old, -jnp.inf)
        s_new = jnp.where(seen_new, s_new, -jnp.inf)
        highest = jnp.maximum(
            jnp.max(s_old, axis=1, keepdims=True), jnp.max(s_new, axis=1, keepdims=True)
        )
        e_old, e_new = jnp.exp(s_old - highest), jnp.exp(s_new - highest)
        inverse = 1.0 / (
            jnp.sum(e_old, axis=1, keepdims=True) + jnp.sum(e_new, axis=1, keepdims=True)
        )
        p_old = (e_old * inverse).astype(jnp.bfloat16)
        p_new = (e_new * inverse).astype(jnp.bfloat16)
        found = jnp.dot(p_old, vc[...], preferred_element_type=jnp.float32) + jnp.dot(
            p_new, vn[...], preferred_element_type=jnp.float32
        )
        found = found.astype(jnp.bfloat16)
        for j in range(per_chunk):
            ctx[side, c, :, j * head_dim : (j + 1) * head_dim] = found[
                j * new_rows : (j + 1) * new_rows
            ]
        if c == 0:
            pl.semaphore_wait(barrier, len(peers))
        ctx_copies.append(
            send(
                ctx.at[side, c], ctx.at[side, c], ctx_send.at[c], ctx_recv.at[c],
                (other, grp, head),
            )
        )

    for load in loads[5:10]:
        load.wait()
    raw = wts[...]
    mixing = (raw / jnp.sum(raw, axis=0, keepdims=True)).astype(jnp.bfloat16).astype(jnp.float32)
    expert = lax.broadcasted_iota(jnp.int32, (LANES, rows_here), 0)
    table = jnp.zeros((LANES, rows_here), jnp.float32)
    for k in range(raw.shape[0]):
        table += jnp.where(ids[k : k + 1, :] == expert, mixing[k : k + 1, :], 0.0)
    unit = (
        lax.broadcasted_iota(jnp.int32, (rows_here, rows_here), 0)
        == lax.broadcasted_iota(jnp.int32, (rows_here, rows_here), 1)
    )
    unit = jnp.where(unit, 1.0, 0.0).astype(jnp.bfloat16)
    table = lax.dot_general(
        unit, table.astype(jnp.bfloat16), NT, preferred_element_type=jnp.float32
    )
    rows[head, side, grp, :, width:] = table.astype(jnp.bfloat16)

    for copy in ctx_copies:
        copy.wait_recv()
    half = wo.shape[1]
    for n in range(0, half, CHUNK):
        total = jnp.zeros((sides * new_rows, CHUNK), jnp.float32)
        for c in range(chunks):
            total += jnp.dot(
                ctx[:, c].reshape(sides * new_rows, CHUNK),
                wo[c * CHUNK : (c + 1) * CHUNK, n : n + CHUNK],
                preferred_element_type=jnp.float32,
            )
        part[:, :, :, n : n + CHUNK] = total.astype(jnp.bfloat16).reshape(
            sides, heads, rows_here, CHUNK
        )
    part_copies = []
    for step in range(heads - 1, -1, -1):
        for turn in range(sides):
            if step == 0 and turn == 0:
                continue
            to_side = side if turn == 0 else other
            slot = turn * heads + step
            part_copies.append(
                send(
                    part.at[to_side, ahead(step)], part_in.at[side, head],
                    part_send.at[slot], part_recv.at[slot], (to_side, grp, ahead(step)),
                )
            )
    part_in[side, head] = part[side, head]
    for copy in part_copies:
        copy.wait_recv()
    square = jnp.zeros((rows_here, 1), jnp.float32)
    for piece in range(sides):
        columns = slice(piece * half, (piece + 1) * half)
        value = hid[:, columns].astype(jnp.float32)
        for j in range(heads):
            value += part_in[piece, j].astype(jnp.float32)
        resid[:, columns] = value
        square += jnp.sum(value * value, axis=1, keepdims=True)
    inv_norm = lax.rsqrt(square * (1.0 / width) + 1e-06)
    rows[head, side, grp, :, :width] = (resid[...] * inv_norm * gain[...]).astype(jnp.bfloat16)

    z_copies, sib_copies = [None] * heads, [[] for _ in range(heads)]
    xy_copies = [[None] * groups for _ in range(heads)]
    ys_copies, ya_copies, yb_copies = [None] * heads, [None] * heads, [None] * heads
    zo_copies = []
    own_expert = side * groups + grp
    many = sides * groups * rows_here

    def axes(step):
        return (1, 2) if step % 2 == 0 else (2, 1)

    def to_group(step, k, origin):
        piece = rows.at[behind(step), side, group(origin)]
        slot = k if origin == 0 else origin ^ k
        xy_copies[step][slot] = send(
            piece, piece, xy_send.at[step, slot], xy_recv.at[step, slot], (side, group(k), head)
        )

    def to_core(step, origin):
        piece = rows.at[behind(step), side, group(origin)]
        sib_copies[step].append(
            send(
                piece, piece, sib_send.at[step, origin], sib_recv.at[step, origin],
                (other, grp, head),
            )
        )

    def spread(step):
        if step > 0:
            z_copies[step].wait_recv()
        first, second = axes(step)
        to_group(step, first, 0)
        to_group(step, second, 0)
        to_core(step, 0)

    def relay(step):
        first, second = axes(step)
        xy_copies[step][first].wait_recv()
        to_group(step, second, first)
        to_core(step, first)
        xy_copies[step][second].wait_recv()
        to_core(step, second)
        xy_copies[step][3].wait_recv()
        to_core(step, 3)

    def experts(step):
        at = behind(step)
        if step == 0:
            for load in loads[10:]:
                load.wait()
        for copy in sib_copies[step]:
            copy.wait_recv()
        x = rows[at, :, :, :, :width].reshape(many, width)
        gate = lax.dot_general(x, wg[...], NT, preferred_element_type=jnp.float32)
        up = lax.dot_general(x, wu[...], NT, preferred_element_type=jnp.float32)
        hidden = (gate / (1.0 + jnp.exp(-gate)) * up).astype(jnp.bfloat16)
        weights = rows[at, :, :, :, width:].reshape(many, LANES).astype(jnp.float32)
        lane = lax.broadcasted_iota(jnp.int32, (many, LANES), 1)
        column = jnp.sum(jnp.where(lane == own_expert, weights, 0.0), axis=1, keepdims=True)
        for n in range(0, width, 2 * CHUNK):
            value = jnp.dot(hidden, wd[:, n : n + 2 * CHUNK], preferred_element_type=jnp.float32)
            value = value.astype(jnp.bfloat16).astype(jnp.float32) * column
            y[at, :, :, :, n : n + 2 * CHUNK] = value.astype(jnp.bfloat16).reshape(
                sides, groups, rows_here, 2 * CHUNK
            )
        ys_copies[step] = send(
            y.at[at, other], y_sib.at[step], ys_send.at[step], ys_recv.at[step],
            (other, grp, head),
        )

    def reduce_cores(step):
        ys_copies[step].wait_recv()
        value = y[behind(step), side].astype(jnp.float32) + y_sib[step].astype(jnp.float32)
        y_sum[step] = value.astype(jnp.bfloat16)
        first, _ = axes(step)
        peer = (side, group(first), head)
        ya_copies[step] = [
            send(
                y_sum.at[step, group(k)], y_a.at[step, i], ya_send.at[step, i],
                ya_recv.at[step, i], peer,
            )
            for i, k in enumerate((3, first))
        ]

    def reduce_first(step):
        ya_copies[step][0].wait_recv()
        _, second = axes(step)
        value = y_sum[step, group(second)].astype(jnp.float32) + y_a[step, 0].astype(jnp.float32)
        y_fwd[step] = value.astype(jnp.bfloat16)
        yb_copies[step] = send(
            y_fwd.at[step], y_b.at[step], yb_send.at[step], yb_recv.at[step],
            (side, group(second), head),
        )

    def reduce_second(step):
        ya_copies[step][1].wait_recv()
        yb_copies[step].wait_recv()
        value = y_sum[step, grp].astype(jnp.float32) + y_a[step, 1].astype(jnp.float32)
        value += y_b[step].astype(jnp.float32)
        if step == 0:
            resid[...] += value
        else:
            z[step] = value.astype(jnp.bfloat16)
            zo_copies.append(
                send(
                    z.at[step], z_in.at[step], zo_send.at[step], zo_recv.at[step],
                    (side, grp, behind(step)),
                )
            )

    block = rows.at[head, side, grp]
    for step in range(1, heads):
        z_copies[step] = send(
            block, block, z_send.at[step], z_recv.at[step], (side, grp, ahead(step))
        )
    later = (reduce_second, reduce_first, reduce_cores, experts, relay)
    for tick in range(heads + len(later)):
        if tick < heads:
            spread(tick)
        for i, stage in enumerate(later):
            step = tick - len(later) + i
            if 0 <= step < heads:
                stage(step)
    value = resid[...]
    for step in range(1, heads):
        zo_copies[step - 1].wait_recv()
        value += z_in[step].astype(jnp.float32)
    out_ref[0] = value.astype(jnp.bfloat16)
    for copy in started:
        copy.wait_send()


def dense_fits(args):
    q_new, hidden_in, expert_ids, w_down = args[0], args[6], args[9], args[13]
    sides, groups, heads = (lax.axis_size(name) for name in ("side", "grp", "head"))
    rows_here, top_k = expert_ids.shape[1:]
    return (
        2 * top_k >= sides * groups
        and sides == 2
        and groups == 4
        and sides * groups <= LANES
        and rows_here % 16 == 0
        and q_new.shape[1] == heads * rows_here
        and q_new.shape[2] % CHUNK == 0
        and hidden_in.shape[2] % (2 * CHUNK) == 0
    )


def shards_dense(
    q_new, k_cache, value_cache, k_new, new_value_rows, cache_len, hidden_in, out_proj, norm_gain,
    expert_ids, gate_wts, w_gate, w_up, w_down,
):
    sides, groups, heads = (lax.axis_size(name) for name in ("side", "grp", "head"))
    new_rows = q_new.shape[1]
    rows_here, width = hidden_in.shape[1:]
    half = out_proj.shape[1]
    chunks = q_new.shape[2] // CHUNK
    operands = (
        q_new, k_cache, value_cache, k_new, new_value_rows, cache_len, hidden_in, out_proj,
        norm_gain.reshape(1, width),
        jnp.swapaxes(expert_ids, 1, 2), jnp.swapaxes(gate_wts, 1, 2),
        jnp.swapaxes(w_gate, 1, 2), jnp.swapaxes(w_up, 1, 2), w_down,
    )
    specs = [pl.BlockSpec(memory_space=pltpu.HBM)] * len(operands)
    specs[5] = pl.BlockSpec(memory_space=pltpu.SMEM)
    bf16 = jnp.bfloat16
    landed = [
        pltpu.VMEM(operands[i].shape[cut:], operands[i].dtype)
        for i, cut in (
            (0, 1), (1, 2), (2, 2), (3, 1), (4, 1), (6, 1), (7, 0), (8, 0), (9, 1), (10, 1),
            (11, 1), (12, 1), (13, 1),
        )
    ]
    dma = pltpu.SemaphoreType.DMA
    return pl.pallas_call(
        dense_kernel,
        out_shape=jax.ShapeDtypeStruct(hidden_in.shape, bf16),
        in_specs=specs,
        out_specs=pl.BlockSpec(memory_space=pltpu.VMEM),
        scratch_shapes=landed
        + [
            pltpu.VMEM((sides, chunks, new_rows, CHUNK), bf16),
            pltpu.VMEM((sides, heads, rows_here, half), bf16),
            pltpu.VMEM((sides, heads, rows_here, half), bf16),
            pltpu.VMEM((rows_here, width), jnp.float32),
            pltpu.VMEM((heads, sides, groups, rows_here, width + LANES), bf16),
            pltpu.VMEM((heads, sides, groups, rows_here, width), bf16),
            pltpu.VMEM((heads, groups, rows_here, width), bf16),
            pltpu.VMEM((heads, groups, rows_here, width), bf16),
            pltpu.VMEM((heads, 2, rows_here, width), bf16),
            pltpu.VMEM((heads, rows_here, width), bf16),
            pltpu.VMEM((heads, rows_here, width), bf16),
            pltpu.VMEM((heads, rows_here, width), bf16),
            pltpu.VMEM((heads, rows_here, width), bf16),
            dma((len(landed),)),
            dma((chunks,)), dma((chunks,)),
            dma((sides * heads,)), dma((sides * heads,)),
            dma((heads,)), dma((heads,)),
            dma((heads, groups)), dma((heads, groups)),
            dma((heads, groups)), dma((heads, groups)),
            dma((heads,)), dma((heads,)),
            dma((heads, 2)), dma((heads, 2)),
            dma((heads,)), dma((heads,)),
            dma((heads,)), dma((heads,)),
        ],
        compiler_params=pltpu.CompilerParams(
            collective_id=0, has_side_effects=True, vmem_limit_bytes=60 * 1024 * 1024
        ),
    )(*operands)


def solution(mesh):
    in_specs = (
        P(("side", "grp"), None, "head"),
        P(("side", "grp"), "head", None, None),
        P(("side", "grp"), "head", None, None),
        P(("side", "grp"), None, "head"),
        P(("side", "grp"), None, "head"),
        P(("side", "grp")),
        P(("side", "grp"), "head", None),
        P("head", "side"),
        P(),
        P(("side", "grp"), "head", None),
        P(("side", "grp"), "head", None),
        P(("side", "grp"), None, "head"),
        P(("side", "grp"), None, "head"),
        P(("side", "grp"), "head", None),
    )
    out_specs = P(("side", "grp"), "head", None)
    def shards(*args):
        if dense_fits(args):
            return shards_dense(*args)
        return shards_sparse(*args)

    return jax.shard_map(shards, mesh=mesh, in_specs=in_specs, out_specs=out_specs, check_vma=False)
```

```python
import math

import jax
import jax.numpy as jnp
from jax import lax
from jax.experimental import pallas as pl
from jax.experimental.pallas import tpu as pltpu
from jax.sharding import PartitionSpec as P

LANES = 128
CHUNK = 256
MESH = pl.DeviceIdType.MESH
NT = (((1,), (1,)), ((), ()))


def attend(q_new, k_cache, value_cache, k_new, new_value_rows, cache_len):
    q_rows = q_new.shape[1]
    head_dim = k_cache.shape[3]
    cached_part = k_cache.shape[2]
    query_groups = q_new.shape[2] // head_dim
    joined_keys = jnp.concatenate([k_cache[0, 0], k_new[0]], axis=0)
    joined_values = jnp.concatenate([value_cache[0, 0], new_value_rows[0]], axis=0)
    query_rows = q_new[0].reshape(q_rows, query_groups, head_dim)
    scores = jnp.einsum(
        "rgd,kd->grk", query_rows, joined_keys, preferred_element_type=jnp.float32
    ) / math.sqrt(head_dim)
    key_pos = jnp.arange(cached_part + q_rows)[None, :]
    row_pos = jnp.arange(q_rows)[:, None]
    visible = jnp.where(
        key_pos < cached_part, key_pos < cache_len[0], key_pos - cached_part <= row_pos
    )
    scores = jnp.where(visible[None], scores, -jnp.inf)
    highest = jnp.max(scores, axis=-1, keepdims=True)
    exp_scores = jnp.exp(scores - highest)
    attn_probs = (exp_scores / jnp.sum(exp_scores, axis=-1, keepdims=True)).astype(jnp.bfloat16)
    context = jnp.einsum(
        "grk,kd->rgd", attn_probs, joined_values, preferred_element_type=jnp.float32
    ).astype(jnp.bfloat16)
    return context.reshape(q_rows, query_groups * head_dim)


def routing_tables(chosen, mixing, experts, most):
    rows_here, top_k = chosen.shape
    one_hot = (
        (chosen[:, :, None] == jnp.arange(experts)[None, None, :])
        .astype(jnp.int32)
        .reshape(rows_here * top_k, experts)
    )
    earlier = jnp.cumsum(one_hot, axis=0) - one_hot
    slot_index = jnp.sum(earlier * one_hot, axis=1)
    target = chosen.reshape(-1) * most + slot_index
    matches = (jnp.arange(experts * most)[:, None] == target[None, :]).reshape(
        experts * most, rows_here, top_k
    )
    dispatch = jnp.any(matches, axis=2).astype(jnp.bfloat16)
    combine = jnp.sum(jnp.where(matches, mixing.astype(jnp.float32)[None], 0.0), axis=2).T.astype(
        jnp.bfloat16
    )
    return (dispatch, combine)


def shards_sparse(
    q_new,
    k_cache,
    value_cache,
    k_new,
    new_value_rows,
    cache_len,
    hidden_in,
    out_proj,
    norm_gain,
    expert_ids,
    gate_wts,
    w_gate,
    w_up,
    w_down,
):
    context = attend(q_new, k_cache, value_cache, k_new, new_value_rows, cache_len)
    width = hidden_in.shape[2]
    halves = jnp.einsum(
        "sre,ec->src",
        lax.all_gather(context[None], "side", axis=0, tiled=True),
        out_proj,
        preferred_element_type=jnp.float32,
    )
    summed = lax.psum_scatter(
        halves.astype(jnp.bfloat16), "head", scatter_dimension=1, tiled=True
    ).astype(jnp.float32)
    attn_out = lax.all_to_all(
        summed.astype(jnp.bfloat16), "side", split_axis=0, concat_axis=2, tiled=True
    ).astype(summed.dtype)[0]
    resid = hidden_in[0].astype(jnp.float32) + attn_out
    normed = (
        resid * lax.rsqrt(jnp.mean(resid * resid, axis=-1, keepdims=True) + 1e-06) * norm_gain
    ).astype(jnp.bfloat16)
    raw_wts = gate_wts[0]
    mixing = (raw_wts / jnp.sum(raw_wts, axis=-1, keepdims=True)).astype(jnp.bfloat16)
    experts = lax.axis_size("side") * lax.axis_size("grp")
    quarters = lax.axis_size("head")
    rows_here = expert_ids.shape[1]
    top_k = expert_ids.shape[2]
    most = max(2, (rows_here * top_k + experts - 1) // experts)
    dispatch, combine = routing_tables(expert_ids[0], mixing, experts, most)
    group_rows, group_dispatch = (
        lax.all_gather(normed[None], "head", axis=0, tiled=True),
        lax.all_gather(dispatch[None], "head", axis=0, tiled=True),
    )
    outgoing = (
        jnp.einsum("hsr,hrd->hsd", group_dispatch, group_rows, preferred_element_type=jnp.float32)
        .astype(jnp.bfloat16)
        .reshape(quarters, experts, most, width)
    )
    slot_rows = lax.all_to_all(outgoing, ("side", "grp"), split_axis=1, concat_axis=1, tiled=True)
    flat_rows = slot_rows.reshape(-1, width)
    gate_proj = jnp.dot(flat_rows, w_gate[0], preferred_element_type=jnp.float32)
    up_proj = jnp.dot(flat_rows, w_up[0], preferred_element_type=jnp.float32)
    hidden = (jax.nn.silu(gate_proj) * up_proj).astype(jnp.bfloat16)
    partial_value = (
        jnp.dot(hidden, w_down[0], preferred_element_type=jnp.float32)
        .astype(jnp.bfloat16)
        .reshape(quarters, experts, most, width)
    )
    combine_all = lax.all_gather(combine[None], "head", axis=0, tiled=True)
    returned = lax.all_to_all(
        partial_value, ("side", "grp"), split_axis=1, concat_axis=1, tiled=True
    )
    weighted = jnp.einsum(
        "hrs,hsd->hrd",
        combine_all,
        returned.reshape(quarters, experts * most, width),
        preferred_element_type=jnp.float32,
    )
    moe_out = lax.psum_scatter(
        weighted.astype(jnp.bfloat16), "head", scatter_dimension=0, tiled=True
    ).astype(jnp.float32)[0]
    return (resid + moe_out).astype(jnp.bfloat16)[None]


def dense_kernel(
    q_hbm, kc_hbm, vc_hbm, kn_hbm, vn_hbm, len_ref, hid_hbm, wo_hbm, gain_hbm, ids_hbm, wts_hbm,
    wg_hbm, wu_hbm, wd_hbm,
    out_ref,
    q, kc, vc, kn, vn, hid, wo, gain, ids, wts, wg, wu, wd,
    ctx, part, part_in, resid, rows, y, y_sib, y_sum, y_a, y_fwd, y_b, z, z_in,
    load_sem, ctx_send, ctx_recv, part_send, part_recv, z_send, z_recv, sib_send, sib_recv,
    xy_send, xy_recv, ys_send, ys_recv, ya_send, ya_recv, yb_send, yb_recv, zo_send, zo_recv,
):
    side, grp, head = lax.axis_index("side"), lax.axis_index("grp"), lax.axis_index("head")
    heads, sides, groups, rows_here, width = y.shape
    other = 1 - side

    def group(k):
        return lax.rem(grp // 2 + k // 2, 2) * 2 + lax.rem(lax.rem(grp, 2) + k % 2, 2)

    def ahead(step):
        return lax.rem(head + step, heads)

    def behind(step):
        return lax.rem(head + heads - step, heads)

    loads = [
        pltpu.make_async_copy(src, dst, load_sem.at[i])
        for i, (src, dst) in enumerate(
            [
                (q_hbm.at[0], q), (kc_hbm.at[0, 0], kc), (kn_hbm.at[0], kn),
                (vc_hbm.at[0, 0], vc), (vn_hbm.at[0], vn), (wo_hbm, wo), (hid_hbm.at[0], hid),
                (gain_hbm, gain), (ids_hbm.at[0], ids), (wts_hbm.at[0], wts),
                (wg_hbm.at[0], wg), (wu_hbm.at[0], wu), (wd_hbm.at[0], wd),
            ]
        )
    ]
    for load in loads[:5]:
        load.start()

    barrier = pltpu.get_barrier_semaphore()
    peers = [(other, grp, head)]
    for step in range(1, heads):
        peers += [(side, grp, ahead(step)), (other, grp, ahead(step))]
    peers += [(side, group(k), head) for k in range(1, groups)]
    for peer in peers:
        pl.semaphore_signal(barrier, inc=1, device_id=peer, device_id_type=MESH)

    started = []

    def send(src, dst, send_sem, recv_sem, peer):
        copy = pltpu.make_async_remote_copy(
            src_ref=src, dst_ref=dst, send_sem=send_sem, recv_sem=recv_sem,
            device_id=peer, device_id_type=MESH,
        )
        copy.start()
        started.append(copy)
        return copy

    head_dim = kn.shape[1]
    new_rows, cached = kn.shape[0], kc.shape[0]
    query_groups = q.shape[1] // head_dim
    half = wo.shape[1]
    scale = 1.0 / math.sqrt(head_dim)
    for load in loads[:5]:
        load.wait()
    for load in loads[5:]:
        load.start()
    valid = len_ref[0]
    many_queries = query_groups * rows_here
    seen_cached = lax.broadcasted_iota(jnp.int32, (many_queries, cached), 1) < valid
    row_pos = lax.rem(lax.broadcasted_iota(jnp.int32, (many_queries, new_rows), 0), rows_here)
    new_pos = lax.broadcasted_iota(jnp.int32, (many_queries, new_rows), 1) - row_pos
    ctx_copies, part_copies = [None] * heads, []

    def attend_rows(step):
        start = pl.multiple_of(ahead(step) * rows_here, rows_here)
        queries = jnp.concatenate(
            [
                q[pl.ds(start, rows_here), j * head_dim : (j + 1) * head_dim]
                for j in range(query_groups)
            ],
            axis=0,
        )
        s_old = lax.dot_general(queries, kc[...], NT, preferred_element_type=jnp.float32) * scale
        s_new = lax.dot_general(queries, kn[...], NT, preferred_element_type=jnp.float32) * scale
        s_old = jnp.where(seen_cached, s_old, -jnp.inf)
        s_new = jnp.where(new_pos <= start, s_new, -jnp.inf)
        highest = jnp.maximum(
            jnp.max(s_old, axis=1, keepdims=True), jnp.max(s_new, axis=1, keepdims=True)
        )
        e_old, e_new = jnp.exp(s_old - highest), jnp.exp(s_new - highest)
        inverse = 1.0 / (
            jnp.sum(e_old, axis=1, keepdims=True) + jnp.sum(e_new, axis=1, keepdims=True)
        )
        p_old = (e_old * inverse).astype(jnp.bfloat16)
        p_new = (e_new * inverse).astype(jnp.bfloat16)
        found = jnp.dot(p_old, vc[...], preferred_element_type=jnp.float32) + jnp.dot(
            p_new, vn[...], preferred_element_type=jnp.float32
        )
        found = found.astype(jnp.bfloat16)
        for j in range(query_groups):
            ctx[side, step, :, j * head_dim : (j + 1) * head_dim] = found[
                j * rows_here : (j + 1) * rows_here
            ]
        if step == heads - 1:
            pl.semaphore_wait(barrier, len(peers))
        ctx_copies[step] = send(
            ctx.at[side, step], ctx.at[side, step], ctx_send.at[step], ctx_recv.at[step],
            (other, grp, head),
        )

    def project_rows(step):
        if step == heads - 1:
            loads[5].wait()
        ctx_copies[step].wait_recv()
        both = ctx[:, step].reshape(sides * rows_here, ctx.shape[3])
        for n in range(0, half, CHUNK):
            total = jnp.dot(both, wo[:, n : n + CHUNK], preferred_element_type=jnp.float32)
            part[:, step, :, n : n + CHUNK] = total.astype(jnp.bfloat16).reshape(
                sides, rows_here, CHUNK
            )
        for turn, to_side in enumerate((side, other)):
            if step == 0 and turn == 0:
                part_in[side, head] = part[side, 0]
                continue
            slot = turn * heads + step
            part_copies.append(
                send(
                    part.at[to_side, step], part_in.at[side, head],
                    part_send.at[slot], part_recv.at[slot], (to_side, grp, ahead(step)),
                )
            )

    attend_rows(heads - 1)
    for step in range(heads - 2, -1, -1):
        attend_rows(step)
        project_rows(step + 1)
    project_rows(0)

    for load in loads[6:10]:
        load.wait()
    raw = wts[...]
    mixing = (raw / jnp.sum(raw, axis=0, keepdims=True)).astype(jnp.bfloat16).astype(jnp.float32)
    expert = lax.broadcasted_iota(jnp.int32, (LANES, rows_here), 0)
    table = jnp.zeros((LANES, rows_here), jnp.float32)
    for k in range(raw.shape[0]):
        table += jnp.where(ids[k : k + 1, :] == expert, mixing[k : k + 1, :], 0.0)
    unit = (
        lax.broadcasted_iota(jnp.int32, (rows_here, rows_here), 0)
        == lax.broadcasted_iota(jnp.int32, (rows_here, rows_here), 1)
    )
    unit = jnp.where(unit, 1.0, 0.0).astype(jnp.bfloat16)
    table = lax.dot_general(
        unit, table.astype(jnp.bfloat16), NT, preferred_element_type=jnp.float32
    )
    rows[head, side, grp, :, width:] = table.astype(jnp.bfloat16)

    for copy in part_copies:
        copy.wait_recv()
    square = jnp.zeros((rows_here, 1), jnp.float32)
    for piece in range(sides):
        columns = slice(piece * half, (piece + 1) * half)
        value = hid[:, columns].astype(jnp.float32)
        for j in range(heads):
            value += part_in[piece, j].astype(jnp.float32)
        resid[:, columns] = value
        square += jnp.sum(value * value, axis=1, keepdims=True)
    inv_norm = lax.rsqrt(square * (1.0 / width) + 1e-06)
    rows[head, side, grp, :, :width] = (resid[...] * inv_norm * gain[...]).astype(jnp.bfloat16)

    z_copies, sib_copies = [None] * heads, [[] for _ in range(heads)]
    xy_copies = [[None] * groups for _ in range(heads)]
    ys_copies, ya_copies, yb_copies = [None] * heads, [None] * heads, [None] * heads
    zo_copies = []
    own_expert = side * groups + grp
    many = sides * groups * rows_here

    def axes(step):
        return (1, 2) if step % 2 == 0 else (2, 1)

    def to_group(step, k, origin):
        piece = rows.at[behind(step), side, group(origin)]
        slot = k if origin == 0 else origin ^ k
        xy_copies[step][slot] = send(
            piece, piece, xy_send.at[step, slot], xy_recv.at[step, slot], (side, group(k), head)
        )

    def to_core(step, origin):
        piece = rows.at[behind(step), side, group(origin)]
        sib_copies[step].append(
            send(
                piece, piece, sib_send.at[step, origin], sib_recv.at[step, origin],
                (other, grp, head),
            )
        )

    def relayed(step):
        return step < heads - 1

    def spread(step):
        if step > 0:
            z_copies[step].wait_recv()
        first, second = axes(step)
        if not relayed(step):
            to_group(step, 3, 0)
        to_group(step, first, 0)
        to_group(step, second, 0)
        to_core(step, 0)

    def relay(step):
        first, second = axes(step)
        xy_copies[step][first].wait_recv()
        if relayed(step):
            to_group(step, second, first)
        to_core(step, first)
        xy_copies[step][second].wait_recv()
        to_core(step, second)

    def finish(step):
        xy_copies[step][3].wait_recv()
        to_core(step, 3)

    def experts(step):
        at = behind(step)
        if step == 0:
            for load in loads[10:]:
                load.wait()
        for copy in sib_copies[step]:
            copy.wait_recv()
        x = rows[at, :, :, :, :width].reshape(many, width)
        gate = lax.dot_general(x, wg[...], NT, preferred_element_type=jnp.float32)
        up = lax.dot_general(x, wu[...], NT, preferred_element_type=jnp.float32)
        hidden = (gate / (1.0 + jnp.exp(-gate)) * up).astype(jnp.bfloat16)
        weights = rows[at, :, :, :, width:].reshape(many, LANES).astype(jnp.float32)
        lane = lax.broadcasted_iota(jnp.int32, (many, LANES), 1)
        column = jnp.sum(jnp.where(lane == own_expert, weights, 0.0), axis=1, keepdims=True)
        for n in range(0, width, 2 * CHUNK):
            value = jnp.dot(hidden, wd[:, n : n + 2 * CHUNK], preferred_element_type=jnp.float32)
            value = value.astype(jnp.bfloat16).astype(jnp.float32) * column
            y[at, :, :, :, n : n + 2 * CHUNK] = value.astype(jnp.bfloat16).reshape(
                sides, groups, rows_here, 2 * CHUNK
            )
        ys_copies[step] = send(
            y.at[at, other], y_sib.at[step], ys_send.at[step], ys_recv.at[step],
            (other, grp, head),
        )

    def reduce_cores(step):
        ys_copies[step].wait_recv()
        value = y[behind(step), side].astype(jnp.float32) + y_sib[step].astype(jnp.float32)
        y_sum[step] = value.astype(jnp.bfloat16)
        first, second = axes(step)
        ya_copies[step] = [
            send(
                y_sum.at[step, group(k)], y_a.at[step, i], ya_send.at[step, i],
                ya_recv.at[step, i], (side, group(first if relayed(step) else k), head),
            )
            for i, k in enumerate((3, first))
        ]
        if not relayed(step):
            yb_copies[step] = send(
                y_sum.at[step, group(second)], y_b.at[step], yb_send.at[step],
                yb_recv.at[step], (side, group(second), head),
            )

    def reduce_first(step):
        ya_copies[step][0].wait_recv()
        if not relayed(step):
            return
        _, second = axes(step)
        value = y_sum[step, group(second)].astype(jnp.float32) + y_a[step, 0].astype(jnp.float32)
        y_fwd[step] = value.astype(jnp.bfloat16)
        yb_copies[step] = send(
            y_fwd.at[step], y_b.at[step], yb_send.at[step], yb_recv.at[step],
            (side, group(second), head),
        )

    def reduce_second(step):
        ya_copies[step][1].wait_recv()
        yb_copies[step].wait_recv()
        value = y_sum[step, grp].astype(jnp.float32) + y_a[step, 1].astype(jnp.float32)
        value += y_b[step].astype(jnp.float32)
        if not relayed(step):
            value += y_a[step, 0].astype(jnp.float32)
        if step == 0:
            resid[...] += value
        else:
            z[step] = value.astype(jnp.bfloat16)
            zo_copies.append(
                send(
                    z.at[step], z_in.at[step], zo_send.at[step], zo_recv.at[step],
                    (side, grp, behind(step)),
                )
            )

    block = rows.at[head, side, grp]
    for step in range(1, heads):
        z_copies[step] = send(
            block, block, z_send.at[step], z_recv.at[step], (side, grp, ahead(step))
        )
    stages = (
        (0, spread), (2, relay), (4, finish), (6, experts), (9, reduce_cores),
        (11, reduce_first), (13, reduce_second),
    )
    for _, _, stage, step in sorted(
        (delay + 2 * step, delay, stage, step)
        for delay, stage in stages
        for step in range(heads)
    ):
        stage(step)
    value = resid[...]
    for step in range(1, heads):
        zo_copies[step - 1].wait_recv()
        value += z_in[step].astype(jnp.float32)
    out_ref[0] = value.astype(jnp.bfloat16)
    for copy in started:
        copy.wait_send()


def dense_fits(args):
    q_new, hidden_in, expert_ids, w_down = args[0], args[6], args[9], args[13]
    sides, groups, heads = (lax.axis_size(name) for name in ("side", "grp", "head"))
    rows_here, top_k = expert_ids.shape[1:]
    return (
        2 * top_k >= sides * groups
        and sides == 2
        and groups == 4
        and sides * groups <= LANES
        and rows_here % 16 == 0
        and q_new.shape[1] == heads * rows_here
        and args[3].shape[2] % LANES == 0
        and args[7].shape[1] % CHUNK == 0
        and hidden_in.shape[2] % (2 * CHUNK) == 0
    )


def shards_dense(
    q_new, k_cache, value_cache, k_new, new_value_rows, cache_len, hidden_in, out_proj, norm_gain,
    expert_ids, gate_wts, w_gate, w_up, w_down,
):
    sides, groups, heads = (lax.axis_size(name) for name in ("side", "grp", "head"))
    rows_here, width = hidden_in.shape[1:]
    half = out_proj.shape[1]
    operands = (
        q_new, k_cache, value_cache, k_new, new_value_rows, cache_len, hidden_in, out_proj,
        norm_gain.reshape(1, width),
        jnp.swapaxes(expert_ids, 1, 2), jnp.swapaxes(gate_wts, 1, 2),
        jnp.swapaxes(w_gate, 1, 2), jnp.swapaxes(w_up, 1, 2), w_down,
    )
    specs = [pl.BlockSpec(memory_space=pltpu.HBM)] * len(operands)
    specs[5] = pl.BlockSpec(memory_space=pltpu.SMEM)
    bf16 = jnp.bfloat16
    landed = [
        pltpu.VMEM(operands[i].shape[cut:], operands[i].dtype)
        for i, cut in (
            (0, 1), (1, 2), (2, 2), (3, 1), (4, 1), (6, 1), (7, 0), (8, 0), (9, 1), (10, 1),
            (11, 1), (12, 1), (13, 1),
        )
    ]
    dma = pltpu.SemaphoreType.DMA
    return pl.pallas_call(
        dense_kernel,
        out_shape=jax.ShapeDtypeStruct(hidden_in.shape, bf16),
        in_specs=specs,
        out_specs=pl.BlockSpec(memory_space=pltpu.VMEM),
        scratch_shapes=landed
        + [
            pltpu.VMEM((sides, heads, rows_here, q_new.shape[2]), bf16),
            pltpu.VMEM((sides, heads, rows_here, half), bf16),
            pltpu.VMEM((sides, heads, rows_here, half), bf16),
            pltpu.VMEM((rows_here, width), jnp.float32),
            pltpu.VMEM((heads, sides, groups, rows_here, width + LANES), bf16),
            pltpu.VMEM((heads, sides, groups, rows_here, width), bf16),
            pltpu.VMEM((heads, groups, rows_here, width), bf16),
            pltpu.VMEM((heads, groups, rows_here, width), bf16),
            pltpu.VMEM((heads, 2, rows_here, width), bf16),
            pltpu.VMEM((heads, rows_here, width), bf16),
            pltpu.VMEM((heads, rows_here, width), bf16),
            pltpu.VMEM((heads, rows_here, width), bf16),
            pltpu.VMEM((heads, rows_here, width), bf16),
            dma((len(landed),)),
            dma((heads,)), dma((heads,)),
            dma((sides * heads,)), dma((sides * heads,)),
            dma((heads,)), dma((heads,)),
            dma((heads, groups)), dma((heads, groups)),
            dma((heads, groups)), dma((heads, groups)),
            dma((heads,)), dma((heads,)),
            dma((heads, 2)), dma((heads, 2)),
            dma((heads,)), dma((heads,)),
            dma((heads,)), dma((heads,)),
        ],
        compiler_params=pltpu.CompilerParams(
            collective_id=0, has_side_effects=True, vmem_limit_bytes=60 * 1024 * 1024
        ),
    )(*operands)


def solution(mesh):
    in_specs = (
        P(("side", "grp"), None, "head"),
        P(("side", "grp"), "head", None, None),
        P(("side", "grp"), "head", None, None),
        P(("side", "grp"), None, "head"),
        P(("side", "grp"), None, "head"),
        P(("side", "grp")),
        P(("side", "grp"), "head", None),
        P("head", "side"),
        P(),
        P(("side", "grp"), "head", None),
        P(("side", "grp"), "head", None),
        P(("side", "grp"), None, "head"),
        P(("side", "grp"), None, "head"),
        P(("side", "grp"), "head", None),
    )
    out_specs = P(("side", "grp"), "head", None)
    def shards(*args):
        if dense_fits(args):
            return shards_dense(*args)
        return shards_sparse(*args)

    return jax.shard_map(shards, mesh=mesh, in_specs=in_specs, out_specs=out_specs, check_vma=False)
```

```python
import math

import jax
import jax.numpy as jnp
from jax import lax
from jax.experimental import pallas as pl
from jax.experimental.pallas import tpu as pltpu
from jax.sharding import PartitionSpec as P

LANES = 128
CHUNK = 256
MESH = pl.DeviceIdType.MESH
NT = (((1,), (1,)), ((), ()))


def attend(q_new, k_cache, value_cache, k_new, new_value_rows, cache_len):
    q_rows = q_new.shape[1]
    head_dim = k_cache.shape[3]
    cached_part = k_cache.shape[2]
    query_groups = q_new.shape[2] // head_dim
    joined_keys = jnp.concatenate([k_cache[0, 0], k_new[0]], axis=0)
    joined_values = jnp.concatenate([value_cache[0, 0], new_value_rows[0]], axis=0)
    query_rows = q_new[0].reshape(q_rows, query_groups, head_dim)
    scores = jnp.einsum(
        "rgd,kd->grk", query_rows, joined_keys, preferred_element_type=jnp.float32
    ) / math.sqrt(head_dim)
    key_pos = jnp.arange(cached_part + q_rows)[None, :]
    row_pos = jnp.arange(q_rows)[:, None]
    visible = jnp.where(
        key_pos < cached_part, key_pos < cache_len[0], key_pos - cached_part <= row_pos
    )
    scores = jnp.where(visible[None], scores, -jnp.inf)
    highest = jnp.max(scores, axis=-1, keepdims=True)
    exp_scores = jnp.exp(scores - highest)
    attn_probs = (exp_scores / jnp.sum(exp_scores, axis=-1, keepdims=True)).astype(jnp.bfloat16)
    context = jnp.einsum(
        "grk,kd->rgd", attn_probs, joined_values, preferred_element_type=jnp.float32
    ).astype(jnp.bfloat16)
    return context.reshape(q_rows, query_groups * head_dim)


def routing_tables(chosen, mixing, experts, most):
    rows_here, top_k = chosen.shape
    one_hot = (
        (chosen[:, :, None] == jnp.arange(experts)[None, None, :])
        .astype(jnp.int32)
        .reshape(rows_here * top_k, experts)
    )
    earlier = jnp.cumsum(one_hot, axis=0) - one_hot
    slot_index = jnp.sum(earlier * one_hot, axis=1)
    target = chosen.reshape(-1) * most + slot_index
    matches = (jnp.arange(experts * most)[:, None] == target[None, :]).reshape(
        experts * most, rows_here, top_k
    )
    dispatch = jnp.any(matches, axis=2).astype(jnp.bfloat16)
    combine = jnp.sum(jnp.where(matches, mixing.astype(jnp.float32)[None], 0.0), axis=2).T.astype(
        jnp.bfloat16
    )
    return (dispatch, combine)


def shards_sparse(
    q_new,
    k_cache,
    value_cache,
    k_new,
    new_value_rows,
    cache_len,
    hidden_in,
    out_proj,
    norm_gain,
    expert_ids,
    gate_wts,
    w_gate,
    w_up,
    w_down,
):
    context = attend(q_new, k_cache, value_cache, k_new, new_value_rows, cache_len)
    width = hidden_in.shape[2]
    halves = jnp.einsum(
        "sre,ec->src",
        lax.all_gather(context[None], "side", axis=0, tiled=True),
        out_proj,
        preferred_element_type=jnp.float32,
    )
    summed = lax.psum_scatter(
        halves.astype(jnp.bfloat16), "head", scatter_dimension=1, tiled=True
    ).astype(jnp.float32)
    attn_out = lax.all_to_all(
        summed.astype(jnp.bfloat16), "side", split_axis=0, concat_axis=2, tiled=True
    ).astype(summed.dtype)[0]
    resid = hidden_in[0].astype(jnp.float32) + attn_out
    normed = (
        resid * lax.rsqrt(jnp.mean(resid * resid, axis=-1, keepdims=True) + 1e-06) * norm_gain
    ).astype(jnp.bfloat16)
    raw_wts = gate_wts[0]
    mixing = (raw_wts / jnp.sum(raw_wts, axis=-1, keepdims=True)).astype(jnp.bfloat16)
    experts = lax.axis_size("side") * lax.axis_size("grp")
    quarters = lax.axis_size("head")
    rows_here = expert_ids.shape[1]
    top_k = expert_ids.shape[2]
    most = max(2, (rows_here * top_k + experts - 1) // experts)
    dispatch, combine = routing_tables(expert_ids[0], mixing, experts, most)
    group_rows, group_dispatch = (
        lax.all_gather(normed[None], "head", axis=0, tiled=True),
        lax.all_gather(dispatch[None], "head", axis=0, tiled=True),
    )
    outgoing = (
        jnp.einsum("hsr,hrd->hsd", group_dispatch, group_rows, preferred_element_type=jnp.float32)
        .astype(jnp.bfloat16)
        .reshape(quarters, experts, most, width)
    )
    slot_rows = lax.all_to_all(outgoing, ("side", "grp"), split_axis=1, concat_axis=1, tiled=True)
    flat_rows = slot_rows.reshape(-1, width)
    gate_proj = jnp.dot(flat_rows, w_gate[0], preferred_element_type=jnp.float32)
    up_proj = jnp.dot(flat_rows, w_up[0], preferred_element_type=jnp.float32)
    hidden = (jax.nn.silu(gate_proj) * up_proj).astype(jnp.bfloat16)
    partial_value = (
        jnp.dot(hidden, w_down[0], preferred_element_type=jnp.float32)
        .astype(jnp.bfloat16)
        .reshape(quarters, experts, most, width)
    )
    combine_all = lax.all_gather(combine[None], "head", axis=0, tiled=True)
    returned = lax.all_to_all(
        partial_value, ("side", "grp"), split_axis=1, concat_axis=1, tiled=True
    )
    weighted = jnp.einsum(
        "hrs,hsd->hrd",
        combine_all,
        returned.reshape(quarters, experts * most, width),
        preferred_element_type=jnp.float32,
    )
    moe_out = lax.psum_scatter(
        weighted.astype(jnp.bfloat16), "head", scatter_dimension=0, tiled=True
    ).astype(jnp.float32)[0]
    return (resid + moe_out).astype(jnp.bfloat16)[None]


def dense_kernel(
    q_hbm, kc_hbm, vc_hbm, kn_hbm, vn_hbm, len_ref, hid_hbm, wo_hbm, gain_hbm, ids_hbm, wts_hbm,
    wg_hbm, wu_hbm, wd_hbm,
    out_ref,
    q, kc, vc, kn, vn, hid, wo, gain, ids, wts, wg, wu, wd,
    ctx, part, part_in, resid, rows, y, y_sib, y_sum, y_a, y_fwd, y_b, z, z_in,
    load_sem, ctx_send, ctx_recv, part_send, part_recv, z_send, z_recv, sib_send, sib_recv,
    xy_send, xy_recv, ys_send, ys_recv, ya_send, ya_recv, yb_send, yb_recv, zo_send, zo_recv,
):
    side, grp, head = lax.axis_index("side"), lax.axis_index("grp"), lax.axis_index("head")
    heads, sides, groups, rows_here, width = y.shape
    other = 1 - side

    def group(k):
        return lax.rem(grp // 2 + k // 2, 2) * 2 + lax.rem(lax.rem(grp, 2) + k % 2, 2)

    def ahead(step):
        return lax.rem(head + step, heads)

    def behind(step):
        return lax.rem(head + heads - step, heads)

    order = sorted(range(heads), key=lambda step: (min(step, heads - step), step))

    loads = [
        pltpu.make_async_copy(src, dst, load_sem.at[i])
        for i, (src, dst) in enumerate(
            [
                (q_hbm.at[0], q), (kc_hbm.at[0, 0], kc), (kn_hbm.at[0], kn),
                (vc_hbm.at[0, 0], vc), (vn_hbm.at[0], vn), (wo_hbm, wo), (hid_hbm.at[0], hid),
                (gain_hbm, gain), (ids_hbm.at[0], ids), (wts_hbm.at[0], wts),
                (wg_hbm.at[0], wg), (wu_hbm.at[0], wu), (wd_hbm.at[0], wd),
            ]
        )
    ]
    for load in loads[:5]:
        load.start()

    barrier = pltpu.get_barrier_semaphore()
    peers = [(other, grp, head)]
    for step in range(1, heads):
        peers += [(side, grp, ahead(step)), (other, grp, ahead(step))]
    peers += [(side, group(k), head) for k in range(1, groups)]
    for peer in peers:
        pl.semaphore_signal(barrier, inc=1, device_id=peer, device_id_type=MESH)

    started = []

    def send(src, dst, send_sem, recv_sem, peer):
        copy = pltpu.make_async_remote_copy(
            src_ref=src, dst_ref=dst, send_sem=send_sem, recv_sem=recv_sem,
            device_id=peer, device_id_type=MESH,
        )
        copy.start()
        started.append(copy)
        return copy

    head_dim = kn.shape[1]
    new_rows, cached = kn.shape[0], kc.shape[0]
    query_groups = q.shape[1] // head_dim
    half = wo.shape[1]
    scale = 1.0 / math.sqrt(head_dim)
    for load in loads[:5]:
        load.wait()
    for load in loads[5:]:
        load.start()
    valid = len_ref[0]
    many_queries = query_groups * rows_here
    seen_cached = lax.broadcasted_iota(jnp.int32, (many_queries, cached), 1) < valid
    row_pos = lax.rem(lax.broadcasted_iota(jnp.int32, (many_queries, new_rows), 0), rows_here)
    new_pos = lax.broadcasted_iota(jnp.int32, (many_queries, new_rows), 1) - row_pos
    ctx_copies, part_copies = [None] * heads, []

    def attend_rows(step):
        start = pl.multiple_of(ahead(step) * rows_here, rows_here)
        queries = jnp.concatenate(
            [
                q[pl.ds(start, rows_here), j * head_dim : (j + 1) * head_dim]
                for j in range(query_groups)
            ],
            axis=0,
        )
        s_old = lax.dot_general(queries, kc[...], NT, preferred_element_type=jnp.float32) * scale
        s_new = lax.dot_general(queries, kn[...], NT, preferred_element_type=jnp.float32) * scale
        s_old = jnp.where(seen_cached, s_old, -jnp.inf)
        s_new = jnp.where(new_pos <= start, s_new, -jnp.inf)
        highest = jnp.maximum(
            jnp.max(s_old, axis=1, keepdims=True), jnp.max(s_new, axis=1, keepdims=True)
        )
        e_old, e_new = jnp.exp(s_old - highest), jnp.exp(s_new - highest)
        inverse = 1.0 / (
            jnp.sum(e_old, axis=1, keepdims=True) + jnp.sum(e_new, axis=1, keepdims=True)
        )
        p_old = (e_old * inverse).astype(jnp.bfloat16)
        p_new = (e_new * inverse).astype(jnp.bfloat16)
        found = jnp.dot(p_old, vc[...], preferred_element_type=jnp.float32) + jnp.dot(
            p_new, vn[...], preferred_element_type=jnp.float32
        )
        found = found.astype(jnp.bfloat16)
        for j in range(query_groups):
            ctx[side, step, :, j * head_dim : (j + 1) * head_dim] = found[
                j * rows_here : (j + 1) * rows_here
            ]
        if step == order[-1]:
            pl.semaphore_wait(barrier, len(peers))
        ctx_copies[step] = send(
            ctx.at[side, step], ctx.at[side, step], ctx_send.at[step], ctx_recv.at[step],
            (other, grp, head),
        )

    def project_rows(step):
        if step == order[-1]:
            loads[5].wait()
        ctx_copies[step].wait_recv()
        both = ctx[:, step].reshape(sides * rows_here, ctx.shape[3])
        for n in range(0, half, CHUNK):
            total = jnp.dot(both, wo[:, n : n + CHUNK], preferred_element_type=jnp.float32)
            part[:, step, :, n : n + CHUNK] = total.astype(jnp.bfloat16).reshape(
                sides, rows_here, CHUNK
            )
        for turn, to_side in enumerate((side, other)):
            if step == 0 and turn == 0:
                part_in[side, head] = part[side, 0]
                continue
            slot = turn * heads + step
            part_copies.append(
                send(
                    part.at[to_side, step], part_in.at[side, head],
                    part_send.at[slot], part_recv.at[slot], (to_side, grp, ahead(step)),
                )
            )

    attend_rows(order[-1])
    for ahead_of, step in zip(order[::-1], order[-2::-1]):
        attend_rows(step)
        project_rows(ahead_of)
    project_rows(order[0])

    for load in loads[6:10]:
        load.wait()
    raw = wts[...]
    mixing = (raw / jnp.sum(raw, axis=0, keepdims=True)).astype(jnp.bfloat16).astype(jnp.float32)
    expert = lax.broadcasted_iota(jnp.int32, (LANES, rows_here), 0)
    table = jnp.zeros((LANES, rows_here), jnp.float32)
    for k in range(raw.shape[0]):
        table += jnp.where(ids[k : k + 1, :] == expert, mixing[k : k + 1, :], 0.0)
    unit = (
        lax.broadcasted_iota(jnp.int32, (rows_here, rows_here), 0)
        == lax.broadcasted_iota(jnp.int32, (rows_here, rows_here), 1)
    )
    unit = jnp.where(unit, 1.0, 0.0).astype(jnp.bfloat16)
    table = lax.dot_general(
        unit, table.astype(jnp.bfloat16), NT, preferred_element_type=jnp.float32
    )
    rows[head, side, grp, :, width:] = table.astype(jnp.bfloat16)

    for copy in part_copies:
        copy.wait_recv()
    square = jnp.zeros((rows_here, 1), jnp.float32)
    for piece in range(sides):
        columns = slice(piece * half, (piece + 1) * half)
        value = hid[:, columns].astype(jnp.float32)
        for j in range(heads):
            value += part_in[piece, j].astype(jnp.float32)
        resid[:, columns] = value
        square += jnp.sum(value * value, axis=1, keepdims=True)
    inv_norm = lax.rsqrt(square * (1.0 / width) + 1e-06)
    rows[head, side, grp, :, :width] = (resid[...] * inv_norm * gain[...]).astype(jnp.bfloat16)

    z_copies, sib_copies = [None] * heads, [[] for _ in range(heads)]
    xy_copies = [[None] * groups for _ in range(heads)]
    ys_copies, ya_copies, yb_copies = [None] * heads, [None] * heads, [None] * heads
    zo_copies = []
    own_expert = side * groups + grp
    many = sides * groups * rows_here

    def axes(step):
        return (1, 2) if order.index(step) % 2 == 0 else (2, 1)

    def to_group(step, k, origin):
        piece = rows.at[behind(step), side, group(origin)]
        slot = k if origin == 0 else origin ^ k
        xy_copies[step][slot] = send(
            piece, piece, xy_send.at[step, slot], xy_recv.at[step, slot], (side, group(k), head)
        )

    def to_core(step, origin):
        piece = rows.at[behind(step), side, group(origin)]
        sib_copies[step].append(
            send(
                piece, piece, sib_send.at[step, origin], sib_recv.at[step, origin],
                (other, grp, head),
            )
        )

    def relayed(step):
        return step != order[-1]

    def spread(step):
        if step > 0:
            z_copies[step].wait_recv()
        first, second = axes(step)
        if not relayed(step):
            to_group(step, 3, 0)
        to_group(step, first, 0)
        to_group(step, second, 0)
        to_core(step, 0)

    def relay(step):
        first, second = axes(step)
        xy_copies[step][first].wait_recv()
        if relayed(step):
            to_group(step, second, first)
        to_core(step, first)
        xy_copies[step][second].wait_recv()
        to_core(step, second)

    def finish(step):
        xy_copies[step][3].wait_recv()
        to_core(step, 3)

    def experts(step):
        at = behind(step)
        if step == 0:
            for load in loads[10:]:
                load.wait()
        for copy in sib_copies[step]:
            copy.wait_recv()
        x = rows[at, :, :, :, :width].reshape(many, width)
        gate = lax.dot_general(x, wg[...], NT, preferred_element_type=jnp.float32)
        up = lax.dot_general(x, wu[...], NT, preferred_element_type=jnp.float32)
        hidden = (gate / (1.0 + jnp.exp(-gate)) * up).astype(jnp.bfloat16)
        weights = rows[at, :, :, :, width:].reshape(many, LANES).astype(jnp.float32)
        lane = lax.broadcasted_iota(jnp.int32, (many, LANES), 1)
        column = jnp.sum(jnp.where(lane == own_expert, weights, 0.0), axis=1, keepdims=True)
        for n in range(0, width, 2 * CHUNK):
            value = jnp.dot(hidden, wd[:, n : n + 2 * CHUNK], preferred_element_type=jnp.float32)
            value = value.astype(jnp.bfloat16).astype(jnp.float32) * column
            y[at, :, :, :, n : n + 2 * CHUNK] = value.astype(jnp.bfloat16).reshape(
                sides, groups, rows_here, 2 * CHUNK
            )
        ys_copies[step] = send(
            y.at[at, other], y_sib.at[step], ys_send.at[step], ys_recv.at[step],
            (other, grp, head),
        )

    def reduce_cores(step):
        ys_copies[step].wait_recv()
        value = y[behind(step), side].astype(jnp.float32) + y_sib[step].astype(jnp.float32)
        y_sum[step] = value.astype(jnp.bfloat16)
        first, second = axes(step)
        ya_copies[step] = [
            send(
                y_sum.at[step, group(k)], y_a.at[step, i], ya_send.at[step, i],
                ya_recv.at[step, i], (side, group(first if relayed(step) else k), head),
            )
            for i, k in enumerate((3, first))
        ]
        if not relayed(step):
            yb_copies[step] = send(
                y_sum.at[step, group(second)], y_b.at[step], yb_send.at[step],
                yb_recv.at[step], (side, group(second), head),
            )

    def reduce_first(step):
        ya_copies[step][0].wait_recv()
        if not relayed(step):
            return
        _, second = axes(step)
        value = y_sum[step, group(second)].astype(jnp.float32) + y_a[step, 0].astype(jnp.float32)
        y_fwd[step] = value.astype(jnp.bfloat16)
        yb_copies[step] = send(
            y_fwd.at[step], y_b.at[step], yb_send.at[step], yb_recv.at[step],
            (side, group(second), head),
        )

    def reduce_second(step):
        ya_copies[step][1].wait_recv()
        yb_copies[step].wait_recv()
        value = y_sum[step, grp].astype(jnp.float32) + y_a[step, 1].astype(jnp.float32)
        value += y_b[step].astype(jnp.float32)
        if not relayed(step):
            value += y_a[step, 0].astype(jnp.float32)
        if step == 0:
            resid[...] += value
        else:
            z[step] = value.astype(jnp.bfloat16)
            zo_copies.append(
                send(
                    z.at[step], z_in.at[step], zo_send.at[step], zo_recv.at[step],
                    (side, grp, behind(step)),
                )
            )

    block = rows.at[head, side, grp]
    for step in order[1:]:
        z_copies[step] = send(
            block, block, z_send.at[step], z_recv.at[step], (side, grp, ahead(step))
        )
    stages = (
        (0, spread), (2, relay), (4, finish), (6, experts), (9, reduce_cores),
        (11, reduce_first), (13, reduce_second),
    )
    for _, _, stage, step in sorted(
        (delay + 2 * turn, delay, stage, step)
        for delay, stage in stages
        for turn, step in enumerate(order)
    ):
        stage(step)
    value = resid[...]
    for step, copy in zip(order[1:], zo_copies):
        copy.wait_recv()
        value += z_in[step].astype(jnp.float32)
    out_ref[0] = value.astype(jnp.bfloat16)
    for copy in started:
        copy.wait_send()


def dense_fits(args):
    q_new, hidden_in, expert_ids, w_down = args[0], args[6], args[9], args[13]
    sides, groups, heads = (lax.axis_size(name) for name in ("side", "grp", "head"))
    rows_here, top_k = expert_ids.shape[1:]
    return (
        2 * top_k >= sides * groups
        and sides == 2
        and groups == 4
        and sides * groups <= LANES
        and rows_here % 16 == 0
        and q_new.shape[1] == heads * rows_here
        and args[3].shape[2] % LANES == 0
        and args[7].shape[1] % CHUNK == 0
        and hidden_in.shape[2] % (2 * CHUNK) == 0
    )


def shards_dense(
    q_new, k_cache, value_cache, k_new, new_value_rows, cache_len, hidden_in, out_proj, norm_gain,
    expert_ids, gate_wts, w_gate, w_up, w_down,
):
    sides, groups, heads = (lax.axis_size(name) for name in ("side", "grp", "head"))
    rows_here, width = hidden_in.shape[1:]
    half = out_proj.shape[1]
    operands = (
        q_new, k_cache, value_cache, k_new, new_value_rows, cache_len, hidden_in, out_proj,
        norm_gain.reshape(1, width),
        jnp.swapaxes(expert_ids, 1, 2), jnp.swapaxes(gate_wts, 1, 2),
        jnp.swapaxes(w_gate, 1, 2), jnp.swapaxes(w_up, 1, 2), w_down,
    )
    specs = [pl.BlockSpec(memory_space=pltpu.HBM)] * len(operands)
    specs[5] = pl.BlockSpec(memory_space=pltpu.SMEM)
    bf16 = jnp.bfloat16
    landed = [
        pltpu.VMEM(operands[i].shape[cut:], operands[i].dtype)
        for i, cut in (
            (0, 1), (1, 2), (2, 2), (3, 1), (4, 1), (6, 1), (7, 0), (8, 0), (9, 1), (10, 1),
            (11, 1), (12, 1), (13, 1),
        )
    ]
    dma = pltpu.SemaphoreType.DMA
    return pl.pallas_call(
        dense_kernel,
        out_shape=pltpu.VMEM(hidden_in.shape, bf16),
        in_specs=specs,
        out_specs=pl.BlockSpec(memory_space=pltpu.VMEM),
        scratch_shapes=landed
        + [
            pltpu.VMEM((sides, heads, rows_here, q_new.shape[2]), bf16),
            pltpu.VMEM((sides, heads, rows_here, half), bf16),
            pltpu.VMEM((sides, heads, rows_here, half), bf16),
            pltpu.VMEM((rows_here, width), jnp.float32),
            pltpu.VMEM((heads, sides, groups, rows_here, width + LANES), bf16),
            pltpu.VMEM((heads, sides, groups, rows_here, width), bf16),
            pltpu.VMEM((heads, groups, rows_here, width), bf16),
            pltpu.VMEM((heads, groups, rows_here, width), bf16),
            pltpu.VMEM((heads, 2, rows_here, width), bf16),
            pltpu.VMEM((heads, rows_here, width), bf16),
            pltpu.VMEM((heads, rows_here, width), bf16),
            pltpu.VMEM((heads, rows_here, width), bf16),
            pltpu.VMEM((heads, rows_here, width), bf16),
            dma((len(landed),)),
            dma((heads,)), dma((heads,)),
            dma((sides * heads,)), dma((sides * heads,)),
            dma((heads,)), dma((heads,)),
            dma((heads, groups)), dma((heads, groups)),
            dma((heads, groups)), dma((heads, groups)),
            dma((heads,)), dma((heads,)),
            dma((heads, 2)), dma((heads, 2)),
            dma((heads,)), dma((heads,)),
            dma((heads,)), dma((heads,)),
        ],
        compiler_params=pltpu.CompilerParams(
            collective_id=0, has_side_effects=True, vmem_limit_bytes=60 * 1024 * 1024
        ),
    )(*operands)


def solution(mesh):
    in_specs = (
        P(("side", "grp"), None, "head"),
        P(("side", "grp"), "head", None, None),
        P(("side", "grp"), "head", None, None),
        P(("side", "grp"), None, "head"),
        P(("side", "grp"), None, "head"),
        P(("side", "grp")),
        P(("side", "grp"), "head", None),
        P("head", "side"),
        P(),
        P(("side", "grp"), "head", None),
        P(("side", "grp"), "head", None),
        P(("side", "grp"), None, "head"),
        P(("side", "grp"), None, "head"),
        P(("side", "grp"), "head", None),
    )
    out_specs = P(("side", "grp"), "head", None)
    def shards(*args):
        if dense_fits(args):
            return shards_dense(*args)
        return shards_sparse(*args)

    return jax.shard_map(shards, mesh=mesh, in_specs=in_specs, out_specs=out_specs, check_vma=False)
```

```python
import math

import jax
import jax.numpy as jnp
from jax import lax
from jax.experimental import pallas as pl
from jax.experimental.pallas import tpu as pltpu
from jax.sharding import PartitionSpec as P

LANES = 128
CHUNK = 256
MESH = pl.DeviceIdType.MESH
NT = (((1,), (1,)), ((), ()))


def attend(q_new, k_cache, value_cache, k_new, new_value_rows, cache_len):
    q_rows = q_new.shape[1]
    head_dim = k_cache.shape[3]
    cached_part = k_cache.shape[2]
    query_groups = q_new.shape[2] // head_dim
    joined_keys = jnp.concatenate([k_cache[0, 0], k_new[0]], axis=0)
    joined_values = jnp.concatenate([value_cache[0, 0], new_value_rows[0]], axis=0)
    query_rows = q_new[0].reshape(q_rows, query_groups, head_dim)
    scores = jnp.einsum(
        "rgd,kd->grk", query_rows, joined_keys, preferred_element_type=jnp.float32
    ) / math.sqrt(head_dim)
    key_pos = jnp.arange(cached_part + q_rows)[None, :]
    row_pos = jnp.arange(q_rows)[:, None]
    visible = jnp.where(
        key_pos < cached_part, key_pos < cache_len[0], key_pos - cached_part <= row_pos
    )
    scores = jnp.where(visible[None], scores, -jnp.inf)
    highest = jnp.max(scores, axis=-1, keepdims=True)
    exp_scores = jnp.exp(scores - highest)
    attn_probs = (exp_scores / jnp.sum(exp_scores, axis=-1, keepdims=True)).astype(jnp.bfloat16)
    context = jnp.einsum(
        "grk,kd->rgd", attn_probs, joined_values, preferred_element_type=jnp.float32
    ).astype(jnp.bfloat16)
    return context.reshape(q_rows, query_groups * head_dim)


def routing_tables(chosen, mixing, experts, most):
    rows_here, top_k = chosen.shape
    one_hot = (
        (chosen[:, :, None] == jnp.arange(experts)[None, None, :])
        .astype(jnp.int32)
        .reshape(rows_here * top_k, experts)
    )
    earlier = jnp.cumsum(one_hot, axis=0) - one_hot
    slot_index = jnp.sum(earlier * one_hot, axis=1)
    target = chosen.reshape(-1) * most + slot_index
    matches = (jnp.arange(experts * most)[:, None] == target[None, :]).reshape(
        experts * most, rows_here, top_k
    )
    dispatch = jnp.any(matches, axis=2).astype(jnp.bfloat16)
    combine = jnp.sum(jnp.where(matches, mixing.astype(jnp.float32)[None], 0.0), axis=2).T.astype(
        jnp.bfloat16
    )
    return (dispatch, combine)


def shards_sparse(
    q_new,
    k_cache,
    value_cache,
    k_new,
    new_value_rows,
    cache_len,
    hidden_in,
    out_proj,
    norm_gain,
    expert_ids,
    gate_wts,
    w_gate,
    w_up,
    w_down,
):
    context = attend(q_new, k_cache, value_cache, k_new, new_value_rows, cache_len)
    width = hidden_in.shape[2]
    halves = jnp.einsum(
        "sre,ec->src",
        lax.all_gather(context[None], "side", axis=0, tiled=True),
        out_proj,
        preferred_element_type=jnp.float32,
    )
    summed = lax.psum_scatter(
        halves.astype(jnp.bfloat16), "head", scatter_dimension=1, tiled=True
    ).astype(jnp.float32)
    attn_out = lax.all_to_all(
        summed.astype(jnp.bfloat16), "side", split_axis=0, concat_axis=2, tiled=True
    ).astype(summed.dtype)[0]
    resid = hidden_in[0].astype(jnp.float32) + attn_out
    normed = (
        resid * lax.rsqrt(jnp.mean(resid * resid, axis=-1, keepdims=True) + 1e-06) * norm_gain
    ).astype(jnp.bfloat16)
    raw_wts = gate_wts[0]
    mixing = (raw_wts / jnp.sum(raw_wts, axis=-1, keepdims=True)).astype(jnp.bfloat16)
    experts = lax.axis_size("side") * lax.axis_size("grp")
    quarters = lax.axis_size("head")
    rows_here = expert_ids.shape[1]
    top_k = expert_ids.shape[2]
    most = max(2, (rows_here * top_k + experts - 1) // experts)
    dispatch, combine = routing_tables(expert_ids[0], mixing, experts, most)
    group_rows, group_dispatch = (
        lax.all_gather(normed[None], "head", axis=0, tiled=True),
        lax.all_gather(dispatch[None], "head", axis=0, tiled=True),
    )
    outgoing = (
        jnp.einsum("hsr,hrd->hsd", group_dispatch, group_rows, preferred_element_type=jnp.float32)
        .astype(jnp.bfloat16)
        .reshape(quarters, experts, most, width)
    )
    slot_rows = lax.all_to_all(outgoing, ("side", "grp"), split_axis=1, concat_axis=1, tiled=True)
    flat_rows = slot_rows.reshape(-1, width)
    gate_proj = jnp.dot(flat_rows, w_gate[0], preferred_element_type=jnp.float32)
    up_proj = jnp.dot(flat_rows, w_up[0], preferred_element_type=jnp.float32)
    hidden = (jax.nn.silu(gate_proj) * up_proj).astype(jnp.bfloat16)
    partial_value = (
        jnp.dot(hidden, w_down[0], preferred_element_type=jnp.float32)
        .astype(jnp.bfloat16)
        .reshape(quarters, experts, most, width)
    )
    combine_all = lax.all_gather(combine[None], "head", axis=0, tiled=True)
    returned = lax.all_to_all(
        partial_value, ("side", "grp"), split_axis=1, concat_axis=1, tiled=True
    )
    weighted = jnp.einsum(
        "hrs,hsd->hrd",
        combine_all,
        returned.reshape(quarters, experts * most, width),
        preferred_element_type=jnp.float32,
    )
    moe_out = lax.psum_scatter(
        weighted.astype(jnp.bfloat16), "head", scatter_dimension=0, tiled=True
    ).astype(jnp.float32)[0]
    return (resid + moe_out).astype(jnp.bfloat16)[None]


def dense_kernel(
    q_hbm, kc_hbm, vc_hbm, kn_hbm, vn_hbm, len_ref, hid_hbm, wo_hbm, gain_hbm, ids_hbm, wts_hbm,
    wg_hbm, wu_hbm, wd_hbm,
    out_ref,
    q, kc, vc, kn, vn, hid, wo, gain, ids, wts, wg, wu, wd,
    ctx, part, part_in, resid, rows, y, y_sib, y_sum, y_a, y_fwd, y_b, z, z_in,
    load_sem, ctx_send, ctx_recv, part_send, part_recv, z_send, z_recv, sib_send, sib_recv,
    xy_send, xy_recv, ys_send, ys_recv, ya_send, ya_recv, yb_send, yb_recv, zo_send, zo_recv,
):
    side, grp, head = lax.axis_index("side"), lax.axis_index("grp"), lax.axis_index("head")
    heads, sides, groups, rows_here, width = y.shape
    other = 1 - side

    def group(k):
        return lax.rem(grp // 2 + k // 2, 2) * 2 + lax.rem(lax.rem(grp, 2) + k % 2, 2)

    def peer(turn):
        total = 0
        for at in range(heads):
            by_distance = sorted(range(heads), key=lambda other_head: abs(other_head - at))
            others = [m for m in range(heads) if m != at]
            weight = math.factorial(heads - 1) // math.prod(at - m for m in others)
            term = weight * by_distance[turn]
            for m in others:
                term = term * (head - m)
            total = total + term
        return total // math.factorial(heads - 1)

    by_turn = [head] + [peer(turn) for turn in range(1, heads)]

    loads = [
        pltpu.make_async_copy(src, dst, load_sem.at[i])
        for i, (src, dst) in enumerate(
            [
                (q_hbm.at[0], q), (kc_hbm.at[0, 0], kc), (kn_hbm.at[0], kn),
                (vc_hbm.at[0, 0], vc), (vn_hbm.at[0], vn), (wo_hbm, wo), (hid_hbm.at[0], hid),
                (gain_hbm, gain), (ids_hbm.at[0], ids), (wts_hbm.at[0], wts),
                (wg_hbm.at[0], wg), (wu_hbm.at[0], wu), (wd_hbm.at[0], wd),
            ]
        )
    ]
    for load in loads[:5]:
        load.start()

    barrier = pltpu.get_barrier_semaphore()
    peers = [(other, grp, head)]
    for step in range(1, heads):
        peers += [(side, grp, by_turn[step]), (other, grp, by_turn[step])]
    peers += [(side, group(k), head) for k in range(1, groups)]
    for peer in peers:
        pl.semaphore_signal(barrier, inc=1, device_id=peer, device_id_type=MESH)

    started = []

    def send(src, dst, send_sem, recv_sem, peer):
        copy = pltpu.make_async_remote_copy(
            src_ref=src, dst_ref=dst, send_sem=send_sem, recv_sem=recv_sem,
            device_id=peer, device_id_type=MESH,
        )
        copy.start()
        started.append(copy)
        return copy

    def arrived(ref, recv_sem):
        pltpu.make_async_remote_copy(
            src_ref=ref, dst_ref=ref, send_sem=recv_sem, recv_sem=recv_sem,
            device_id=(other, grp, head), device_id_type=MESH,
        ).wait_recv()

    head_dim = kn.shape[1]
    new_rows, cached = kn.shape[0], kc.shape[0]
    query_groups = q.shape[1] // head_dim
    half = wo.shape[1]
    scale = 1.0 / math.sqrt(head_dim)
    for load in loads[:5]:
        load.wait()
    for load in loads[5:]:
        load.start()
    valid = len_ref[0]
    many_queries = query_groups * rows_here
    seen_cached = lax.broadcasted_iota(jnp.int32, (many_queries, cached), 1) < valid
    row_pos = lax.rem(lax.broadcasted_iota(jnp.int32, (many_queries, new_rows), 0), rows_here)
    new_pos = lax.broadcasted_iota(jnp.int32, (many_queries, new_rows), 1) - row_pos
    ctx_copies = [None] * heads

    def attend_rows(step):
        start = pl.multiple_of(by_turn[step] * rows_here, rows_here)
        queries = jnp.concatenate(
            [
                q[pl.ds(start, rows_here), j * head_dim : (j + 1) * head_dim]
                for j in range(query_groups)
            ],
            axis=0,
        )
        s_old = lax.dot_general(queries, kc[...], NT, preferred_element_type=jnp.float32) * scale
        s_new = lax.dot_general(queries, kn[...], NT, preferred_element_type=jnp.float32) * scale
        s_old = jnp.where(seen_cached, s_old, -jnp.inf)
        s_new = jnp.where(new_pos <= start, s_new, -jnp.inf)
        highest = jnp.maximum(
            jnp.max(s_old, axis=1, keepdims=True), jnp.max(s_new, axis=1, keepdims=True)
        )
        e_old, e_new = jnp.exp(s_old - highest), jnp.exp(s_new - highest)
        inverse = 1.0 / (
            jnp.sum(e_old, axis=1, keepdims=True) + jnp.sum(e_new, axis=1, keepdims=True)
        )
        p_old = (e_old * inverse).astype(jnp.bfloat16)
        p_new = (e_new * inverse).astype(jnp.bfloat16)
        found = jnp.dot(p_old, vc[...], preferred_element_type=jnp.float32) + jnp.dot(
            p_new, vn[...], preferred_element_type=jnp.float32
        )
        found = found.astype(jnp.bfloat16)
        for j in range(query_groups):
            ctx[side, step, :, j * head_dim : (j + 1) * head_dim] = found[
                j * rows_here : (j + 1) * rows_here
            ]
        if step == heads - 1:
            pl.semaphore_wait(barrier, len(peers))
        ctx_copies[step] = send(
            ctx.at[side, step], ctx.at[side, step], ctx_send.at[step], ctx_recv.at[step],
            (other, grp, head),
        )

    def project_rows(step):
        if step == heads - 1:
            loads[5].wait()
        ctx_copies[step].wait_recv()
        both = ctx[:, step].reshape(sides * rows_here, ctx.shape[3])
        for n in range(0, half, CHUNK):
            total = jnp.dot(both, wo[:, n : n + CHUNK], preferred_element_type=jnp.float32)
            part[:, step, :, n : n + CHUNK] = total.astype(jnp.bfloat16).reshape(
                sides, rows_here, CHUNK
            )
        for turn, to_side in enumerate((side, other)):
            if step == 0 and turn == 0:
                part_in[side, head] = part[side, 0]
                continue
            slot = turn * heads + step
            send(
                part.at[to_side, step], part_in.at[side, head], part_send.at[slot],
                part_recv.at[turn * heads + head], (to_side, grp, by_turn[step]),
            )

    attend_rows(heads - 1)
    for step in range(heads - 2, -1, -1):
        attend_rows(step)
        project_rows(step + 1)
    project_rows(0)

    for load in loads[6:10]:
        load.wait()
    raw = wts[...]
    mixing = (raw / jnp.sum(raw, axis=0, keepdims=True)).astype(jnp.bfloat16).astype(jnp.float32)
    expert = lax.broadcasted_iota(jnp.int32, (LANES, rows_here), 0)
    table = jnp.zeros((LANES, rows_here), jnp.float32)
    for k in range(raw.shape[0]):
        table += jnp.where(ids[k : k + 1, :] == expert, mixing[k : k + 1, :], 0.0)
    unit = (
        lax.broadcasted_iota(jnp.int32, (rows_here, rows_here), 0)
        == lax.broadcasted_iota(jnp.int32, (rows_here, rows_here), 1)
    )
    unit = jnp.where(unit, 1.0, 0.0).astype(jnp.bfloat16)
    table = lax.dot_general(
        unit, table.astype(jnp.bfloat16), NT, preferred_element_type=jnp.float32
    )
    rows[head, side, grp, :, width:] = table.astype(jnp.bfloat16)

    for step in range(heads):
        arrived(part_in.at[other, by_turn[step]], part_recv.at[heads + by_turn[step]])
        if step > 0:
            arrived(part_in.at[side, by_turn[step]], part_recv.at[by_turn[step]])
    square = jnp.zeros((rows_here, 1), jnp.float32)
    for piece in range(sides):
        columns = slice(piece * half, (piece + 1) * half)
        value = hid[:, columns].astype(jnp.float32)
        for j in range(heads):
            value += part_in[piece, j].astype(jnp.float32)
        resid[:, columns] = value
        square += jnp.sum(value * value, axis=1, keepdims=True)
    inv_norm = lax.rsqrt(square * (1.0 / width) + 1e-06)
    rows[head, side, grp, :, :width] = (resid[...] * inv_norm * gain[...]).astype(jnp.bfloat16)

    sib_copies = [[] for _ in range(heads)]
    xy_copies = [[None] * groups for _ in range(heads)]
    ys_copies, ya_copies, yb_copies = [None] * heads, [None] * heads, [None] * heads
    own_expert = side * groups + grp
    many = sides * groups * rows_here

    def axes(step):
        return (1, 2) if step % 2 == 0 else (2, 1)

    def to_group(step, k, origin):
        piece = rows.at[by_turn[step], side, group(origin)]
        slot = k if origin == 0 else origin ^ k
        xy_copies[step][slot] = send(
            piece, piece, xy_send.at[step, slot], xy_recv.at[step, slot], (side, group(k), head)
        )

    def to_core(step, origin):
        piece = rows.at[by_turn[step], side, group(origin)]
        sib_copies[step].append(
            send(
                piece, piece, sib_send.at[step, origin], sib_recv.at[step, origin],
                (other, grp, head),
            )
        )

    def relayed(step):
        return step < heads // 2

    def spread(step):
        if step > 0:
            arrived(rows.at[by_turn[step], side, grp], z_recv.at[by_turn[step]])
        first, second = axes(step)
        if not relayed(step):
            to_group(step, 3, 0)
        to_group(step, first, 0)
        to_group(step, second, 0)
        to_core(step, 0)

    def relay(step):
        first, second = axes(step)
        xy_copies[step][first].wait_recv()
        if relayed(step):
            to_group(step, second, first)
        to_core(step, first)
        xy_copies[step][second].wait_recv()
        to_core(step, second)

    def finish(step):
        xy_copies[step][3].wait_recv()
        to_core(step, 3)

    def experts(step):
        at = by_turn[step]
        if step == 0:
            for load in loads[10:]:
                load.wait()
        for copy in sib_copies[step]:
            copy.wait_recv()
        x = rows[at, :, :, :, :width].reshape(many, width)
        gate = lax.dot_general(x, wg[...], NT, preferred_element_type=jnp.float32)
        up = lax.dot_general(x, wu[...], NT, preferred_element_type=jnp.float32)
        hidden = (gate / (1.0 + jnp.exp(-gate)) * up).astype(jnp.bfloat16)
        weights = rows[at, :, :, :, width:].reshape(many, LANES).astype(jnp.float32)
        lane = lax.broadcasted_iota(jnp.int32, (many, LANES), 1)
        column = jnp.sum(jnp.where(lane == own_expert, weights, 0.0), axis=1, keepdims=True)
        for n in range(0, width, 2 * CHUNK):
            value = jnp.dot(hidden, wd[:, n : n + 2 * CHUNK], preferred_element_type=jnp.float32)
            value = value.astype(jnp.bfloat16).astype(jnp.float32) * column
            y[at, :, :, :, n : n + 2 * CHUNK] = value.astype(jnp.bfloat16).reshape(
                sides, groups, rows_here, 2 * CHUNK
            )
        ys_copies[step] = send(
            y.at[at, other], y_sib.at[step], ys_send.at[step], ys_recv.at[step],
            (other, grp, head),
        )

    def reduce_cores(step):
        ys_copies[step].wait_recv()
        value = y[by_turn[step], side].astype(jnp.float32) + y_sib[step].astype(jnp.float32)
        y_sum[step] = value.astype(jnp.bfloat16)
        first, second = axes(step)
        ya_copies[step] = [
            send(
                y_sum.at[step, group(k)], y_a.at[step, i], ya_send.at[step, i],
                ya_recv.at[step, i], (side, group(first if relayed(step) else k), head),
            )
            for i, k in enumerate((3, first))
        ]
        if not relayed(step):
            yb_copies[step] = send(
                y_sum.at[step, group(second)], y_b.at[step], yb_send.at[step],
                yb_recv.at[step], (side, group(second), head),
            )

    def reduce_first(step):
        ya_copies[step][0].wait_recv()
        if not relayed(step):
            return
        _, second = axes(step)
        value = y_sum[step, group(second)].astype(jnp.float32) + y_a[step, 0].astype(jnp.float32)
        y_fwd[step] = value.astype(jnp.bfloat16)
        yb_copies[step] = send(
            y_fwd.at[step], y_b.at[step], yb_send.at[step], yb_recv.at[step],
            (side, group(second), head),
        )

    def reduce_second(step):
        ya_copies[step][1].wait_recv()
        yb_copies[step].wait_recv()
        value = y_sum[step, grp].astype(jnp.float32) + y_a[step, 1].astype(jnp.float32)
        value += y_b[step].astype(jnp.float32)
        if not relayed(step):
            value += y_a[step, 0].astype(jnp.float32)
        if step == 0:
            resid[...] += value
        else:
            z[step] = value.astype(jnp.bfloat16)
            send(
                z.at[step], z_in.at[head], zo_send.at[step], zo_recv.at[head],
                (side, grp, by_turn[step]),
            )

    block = rows.at[head, side, grp]
    for step in range(1, heads):
        send(block, block, z_send.at[step], z_recv.at[head], (side, grp, by_turn[step]))
    stages = (
        (0, spread), (2, relay), (4, finish), (6, experts), (9, reduce_cores),
        (11, reduce_first), (13, reduce_second),
    )
    for _, _, stage, step in sorted(
        (delay + 2 * step, delay, stage, step)
        for delay, stage in stages
        for step in range(heads)
    ):
        stage(step)
    value = resid[...]
    for step in range(1, heads):
        arrived(z_in.at[by_turn[step]], zo_recv.at[by_turn[step]])
        value += z_in[by_turn[step]].astype(jnp.float32)
    out_ref[0] = value.astype(jnp.bfloat16)
    for copy in started:
        copy.wait_send()


def dense_fits(args):
    q_new, hidden_in, expert_ids, w_down = args[0], args[6], args[9], args[13]
    sides, groups, heads = (lax.axis_size(name) for name in ("side", "grp", "head"))
    rows_here, top_k = expert_ids.shape[1:]
    return (
        2 * top_k >= sides * groups
        and sides == 2
        and groups == 4
        and sides * groups <= LANES
        and rows_here % 16 == 0
        and q_new.shape[1] == heads * rows_here
        and args[3].shape[2] % LANES == 0
        and args[7].shape[1] % CHUNK == 0
        and hidden_in.shape[2] % (2 * CHUNK) == 0
    )


def shards_dense(
    q_new, k_cache, value_cache, k_new, new_value_rows, cache_len, hidden_in, out_proj, norm_gain,
    expert_ids, gate_wts, w_gate, w_up, w_down,
):
    sides, groups, heads = (lax.axis_size(name) for name in ("side", "grp", "head"))
    rows_here, width = hidden_in.shape[1:]
    half = out_proj.shape[1]
    operands = (
        q_new, k_cache, value_cache, k_new, new_value_rows, cache_len, hidden_in, out_proj,
        norm_gain.reshape(1, width),
        jnp.swapaxes(expert_ids, 1, 2), jnp.swapaxes(gate_wts, 1, 2),
        jnp.swapaxes(w_gate, 1, 2), jnp.swapaxes(w_up, 1, 2), w_down,
    )
    specs = [pl.BlockSpec(memory_space=pltpu.HBM)] * len(operands)
    specs[5] = pl.BlockSpec(memory_space=pltpu.SMEM)
    bf16 = jnp.bfloat16
    landed = [
        pltpu.VMEM(operands[i].shape[cut:], operands[i].dtype)
        for i, cut in (
            (0, 1), (1, 2), (2, 2), (3, 1), (4, 1), (6, 1), (7, 0), (8, 0), (9, 1), (10, 1),
            (11, 1), (12, 1), (13, 1),
        )
    ]
    dma = pltpu.SemaphoreType.DMA
    return pl.pallas_call(
        dense_kernel,
        out_shape=pltpu.VMEM(hidden_in.shape, bf16),
        in_specs=specs,
        out_specs=pl.BlockSpec(memory_space=pltpu.VMEM),
        scratch_shapes=landed
        + [
            pltpu.VMEM((sides, heads, rows_here, q_new.shape[2]), bf16),
            pltpu.VMEM((sides, heads, rows_here, half), bf16),
            pltpu.VMEM((sides, heads, rows_here, half), bf16),
            pltpu.VMEM((rows_here, width), jnp.float32),
            pltpu.VMEM((heads, sides, groups, rows_here, width + LANES), bf16),
            pltpu.VMEM((heads, sides, groups, rows_here, width), bf16),
            pltpu.VMEM((heads, groups, rows_here, width), bf16),
            pltpu.VMEM((heads, groups, rows_here, width), bf16),
            pltpu.VMEM((heads, 2, rows_here, width), bf16),
            pltpu.VMEM((heads, rows_here, width), bf16),
            pltpu.VMEM((heads, rows_here, width), bf16),
            pltpu.VMEM((heads, rows_here, width), bf16),
            pltpu.VMEM((heads, rows_here, width), bf16),
            dma((len(landed),)),
            dma((heads,)), dma((heads,)),
            dma((sides * heads,)), dma((sides * heads,)),
            dma((heads,)), dma((heads,)),
            dma((heads, groups)), dma((heads, groups)),
            dma((heads, groups)), dma((heads, groups)),
            dma((heads,)), dma((heads,)),
            dma((heads, 2)), dma((heads, 2)),
            dma((heads,)), dma((heads,)),
            dma((heads,)), dma((heads,)),
        ],
        compiler_params=pltpu.CompilerParams(
            collective_id=0, has_side_effects=True, vmem_limit_bytes=60 * 1024 * 1024
        ),
    )(*operands)


def solution(mesh):
    in_specs = (
        P(("side", "grp"), None, "head"),
        P(("side", "grp"), "head", None, None),
        P(("side", "grp"), "head", None, None),
        P(("side", "grp"), None, "head"),
        P(("side", "grp"), None, "head"),
        P(("side", "grp")),
        P(("side", "grp"), "head", None),
        P("head", "side"),
        P(),
        P(("side", "grp"), "head", None),
        P(("side", "grp"), "head", None),
        P(("side", "grp"), None, "head"),
        P(("side", "grp"), None, "head"),
        P(("side", "grp"), "head", None),
    )
    out_specs = P(("side", "grp"), "head", None)
    def shards(*args):
        if dense_fits(args):
            return shards_dense(*args)
        return shards_sparse(*args)

    return jax.shard_map(shards, mesh=mesh, in_specs=in_specs, out_specs=out_specs, check_vma=False)
```

```python
import math

import jax
import jax.numpy as jnp
from jax import lax
from jax.experimental import pallas as pl
from jax.experimental.pallas import tpu as pltpu
from jax.sharding import PartitionSpec as P

LANES = 128
CHUNK = 256
MESH = pl.DeviceIdType.MESH
NT = (((1,), (1,)), ((), ()))


def attend(q_new, k_cache, value_cache, k_new, new_value_rows, cache_len):
    q_rows = q_new.shape[1]
    head_dim = k_cache.shape[3]
    cached_part = k_cache.shape[2]
    query_groups = q_new.shape[2] // head_dim
    joined_keys = jnp.concatenate([k_cache[0, 0], k_new[0]], axis=0)
    joined_values = jnp.concatenate([value_cache[0, 0], new_value_rows[0]], axis=0)
    query_rows = q_new[0].reshape(q_rows, query_groups, head_dim)
    scores = jnp.einsum(
        "rgd,kd->grk", query_rows, joined_keys, preferred_element_type=jnp.float32
    ) / math.sqrt(head_dim)
    key_pos = jnp.arange(cached_part + q_rows)[None, :]
    row_pos = jnp.arange(q_rows)[:, None]
    visible = jnp.where(
        key_pos < cached_part, key_pos < cache_len[0], key_pos - cached_part <= row_pos
    )
    scores = jnp.where(visible[None], scores, -jnp.inf)
    highest = jnp.max(scores, axis=-1, keepdims=True)
    exp_scores = jnp.exp(scores - highest)
    attn_probs = (exp_scores / jnp.sum(exp_scores, axis=-1, keepdims=True)).astype(jnp.bfloat16)
    context = jnp.einsum(
        "grk,kd->rgd", attn_probs, joined_values, preferred_element_type=jnp.float32
    ).astype(jnp.bfloat16)
    return context.reshape(q_rows, query_groups * head_dim)


def routing_tables(chosen, mixing, experts, most):
    rows_here, top_k = chosen.shape
    one_hot = (
        (chosen[:, :, None] == jnp.arange(experts)[None, None, :])
        .astype(jnp.int32)
        .reshape(rows_here * top_k, experts)
    )
    earlier = jnp.cumsum(one_hot, axis=0) - one_hot
    slot_index = jnp.sum(earlier * one_hot, axis=1)
    target = chosen.reshape(-1) * most + slot_index
    matches = (jnp.arange(experts * most)[:, None] == target[None, :]).reshape(
        experts * most, rows_here, top_k
    )
    dispatch = jnp.any(matches, axis=2).astype(jnp.bfloat16)
    combine = jnp.sum(jnp.where(matches, mixing.astype(jnp.float32)[None], 0.0), axis=2).T.astype(
        jnp.bfloat16
    )
    return (dispatch, combine)


def shards_sparse(
    q_new,
    k_cache,
    value_cache,
    k_new,
    new_value_rows,
    cache_len,
    hidden_in,
    out_proj,
    norm_gain,
    expert_ids,
    gate_wts,
    w_gate,
    w_up,
    w_down,
):
    context = attend(q_new, k_cache, value_cache, k_new, new_value_rows, cache_len)
    width = hidden_in.shape[2]
    halves = jnp.einsum(
        "sre,ec->src",
        lax.all_gather(context[None], "side", axis=0, tiled=True),
        out_proj,
        preferred_element_type=jnp.float32,
    )
    summed = lax.psum_scatter(
        halves.astype(jnp.bfloat16), "head", scatter_dimension=1, tiled=True
    ).astype(jnp.float32)
    attn_out = lax.all_to_all(
        summed.astype(jnp.bfloat16), "side", split_axis=0, concat_axis=2, tiled=True
    ).astype(summed.dtype)[0]
    resid = hidden_in[0].astype(jnp.float32) + attn_out
    normed = (
        resid * lax.rsqrt(jnp.mean(resid * resid, axis=-1, keepdims=True) + 1e-06) * norm_gain
    ).astype(jnp.bfloat16)
    raw_wts = gate_wts[0]
    mixing = (raw_wts / jnp.sum(raw_wts, axis=-1, keepdims=True)).astype(jnp.bfloat16)
    experts = lax.axis_size("side") * lax.axis_size("grp")
    quarters = lax.axis_size("head")
    rows_here = expert_ids.shape[1]
    top_k = expert_ids.shape[2]
    most = max(2, (rows_here * top_k + experts - 1) // experts)
    dispatch, combine = routing_tables(expert_ids[0], mixing, experts, most)
    group_rows, group_dispatch = (
        lax.all_gather(normed[None], "head", axis=0, tiled=True),
        lax.all_gather(dispatch[None], "head", axis=0, tiled=True),
    )
    outgoing = (
        jnp.einsum("hsr,hrd->hsd", group_dispatch, group_rows, preferred_element_type=jnp.float32)
        .astype(jnp.bfloat16)
        .reshape(quarters, experts, most, width)
    )
    slot_rows = lax.all_to_all(outgoing, ("side", "grp"), split_axis=1, concat_axis=1, tiled=True)
    flat_rows = slot_rows.reshape(-1, width)
    gate_proj = jnp.dot(flat_rows, w_gate[0], preferred_element_type=jnp.float32)
    up_proj = jnp.dot(flat_rows, w_up[0], preferred_element_type=jnp.float32)
    hidden = (jax.nn.silu(gate_proj) * up_proj).astype(jnp.bfloat16)
    partial_value = (
        jnp.dot(hidden, w_down[0], preferred_element_type=jnp.float32)
        .astype(jnp.bfloat16)
        .reshape(quarters, experts, most, width)
    )
    combine_all = lax.all_gather(combine[None], "head", axis=0, tiled=True)
    returned = lax.all_to_all(
        partial_value, ("side", "grp"), split_axis=1, concat_axis=1, tiled=True
    )
    weighted = jnp.einsum(
        "hrs,hsd->hrd",
        combine_all,
        returned.reshape(quarters, experts * most, width),
        preferred_element_type=jnp.float32,
    )
    moe_out = lax.psum_scatter(
        weighted.astype(jnp.bfloat16), "head", scatter_dimension=0, tiled=True
    ).astype(jnp.float32)[0]
    return (resid + moe_out).astype(jnp.bfloat16)[None]


def dense_kernel(
    q_hbm, kc_hbm, vc_hbm, kn_hbm, vn_hbm, len_ref, hid_hbm, wo_hbm, gain_hbm, ids_hbm, wts_hbm,
    wg_hbm, wu_hbm, wd_hbm,
    out_ref,
    q, kc, vc, kn, vn, hid, wo, gain, ids, wts, wg, wu, wd,
    ctx, part, part_in, resid, rows, y, y_sib, y_sum, y_a, y_fwd, y_b, z, z_in,
    load_sem, ctx_send, ctx_recv, part_send, part_recv, z_send, z_recv, sib_send, sib_recv,
    xy_send, xy_recv, ys_send, ys_recv, ya_send, ya_recv, yb_send, yb_recv, zo_send, zo_recv,
):
    side, grp, head = lax.axis_index("side"), lax.axis_index("grp"), lax.axis_index("head")
    heads, sides, groups, rows_here, width = y.shape
    other = 1 - side

    def group(k):
        return lax.rem(grp // 2 + k // 2, 2) * 2 + lax.rem(lax.rem(grp, 2) + k % 2, 2)

    def ahead(step):
        return lax.rem(head + step, heads)

    def behind(step):
        return lax.rem(head + heads - step, heads)

    order = sorted(range(heads), key=lambda step: (min(step, heads - step), step))

    loads = [
        pltpu.make_async_copy(src, dst, load_sem.at[i])
        for i, (src, dst) in enumerate(
            [
                (q_hbm.at[0], q), (kc_hbm.at[0, 0], kc), (kn_hbm.at[0], kn),
                (vc_hbm.at[0, 0], vc), (vn_hbm.at[0], vn), (wo_hbm, wo), (hid_hbm.at[0], hid),
                (gain_hbm, gain), (ids_hbm.at[0], ids), (wts_hbm.at[0], wts),
                (wg_hbm.at[0], wg), (wu_hbm.at[0], wu), (wd_hbm.at[0], wd),
            ]
        )
    ]
    for load in loads[:5]:
        load.start()

    barrier = pltpu.get_barrier_semaphore()
    peers = [(other, grp, head)]
    for step in range(1, heads):
        peers += [(side, grp, ahead(step)), (other, grp, ahead(step))]
    peers += [(side, group(1), head), (side, group(2), head)]
    for peer in peers:
        pl.semaphore_signal(barrier, inc=1, device_id=peer, device_id_type=MESH)

    started = []

    def send(src, dst, send_sem, recv_sem, peer):
        copy = pltpu.make_async_remote_copy(
            src_ref=src, dst_ref=dst, send_sem=send_sem, recv_sem=recv_sem,
            device_id=peer, device_id_type=MESH,
        )
        copy.start()
        started.append(copy)
        return copy

    head_dim = kn.shape[1]
    new_rows, cached = kn.shape[0], kc.shape[0]
    query_groups = q.shape[1] // head_dim
    half = wo.shape[1]
    scale = 1.0 / math.sqrt(head_dim)
    for load in loads[:5]:
        load.wait()
    for load in loads[5:]:
        load.start()
    valid = len_ref[0]
    many_queries = query_groups * rows_here
    seen_cached = lax.broadcasted_iota(jnp.int32, (many_queries, cached), 1) < valid
    row_pos = lax.rem(lax.broadcasted_iota(jnp.int32, (many_queries, new_rows), 0), rows_here)
    new_pos = lax.broadcasted_iota(jnp.int32, (many_queries, new_rows), 1) - row_pos
    ctx_copies, part_copies = [None] * heads, []

    def attend_rows(step):
        start = pl.multiple_of(ahead(step) * rows_here, rows_here)
        queries = jnp.concatenate(
            [
                q[pl.ds(start, rows_here), j * head_dim : (j + 1) * head_dim]
                for j in range(query_groups)
            ],
            axis=0,
        )
        s_old = lax.dot_general(queries, kc[...], NT, preferred_element_type=jnp.float32) * scale
        s_new = lax.dot_general(queries, kn[...], NT, preferred_element_type=jnp.float32) * scale
        s_old = jnp.where(seen_cached, s_old, -jnp.inf)
        s_new = jnp.where(new_pos <= start, s_new, -jnp.inf)
        highest = jnp.maximum(
            jnp.max(s_old, axis=1, keepdims=True), jnp.max(s_new, axis=1, keepdims=True)
        )
        e_old, e_new = jnp.exp(s_old - highest), jnp.exp(s_new - highest)
        inverse = 1.0 / (
            jnp.sum(e_old, axis=1, keepdims=True) + jnp.sum(e_new, axis=1, keepdims=True)
        )
        p_old = (e_old * inverse).astype(jnp.bfloat16)
        p_new = (e_new * inverse).astype(jnp.bfloat16)
        found = jnp.dot(p_old, vc[...], preferred_element_type=jnp.float32) + jnp.dot(
            p_new, vn[...], preferred_element_type=jnp.float32
        )
        found = found.astype(jnp.bfloat16)
        for j in range(query_groups):
            ctx[side, step, :, j * head_dim : (j + 1) * head_dim] = found[
                j * rows_here : (j + 1) * rows_here
            ]
        if step == order[-1]:
            pl.semaphore_wait(barrier, len(peers))
        ctx_copies[step] = send(
            ctx.at[side, step], ctx.at[side, step], ctx_send.at[step], ctx_recv.at[step],
            (other, grp, head),
        )

    def project_rows(step):
        if step == order[-1]:
            loads[5].wait()
        ctx_copies[step].wait_recv()
        both = ctx[:, step].reshape(sides * rows_here, ctx.shape[3])
        for n in range(0, half, CHUNK):
            total = jnp.dot(both, wo[:, n : n + CHUNK], preferred_element_type=jnp.float32)
            part[:, step, :, n : n + CHUNK] = total.astype(jnp.bfloat16).reshape(
                sides, rows_here, CHUNK
            )
        for turn, to_side in enumerate((side, other)):
            if step == 0 and turn == 0:
                part_in[side, head] = part[side, 0]
                continue
            slot = turn * heads + step
            part_copies.append(
                send(
                    part.at[to_side, step], part_in.at[side, head],
                    part_send.at[slot], part_recv.at[slot], (to_side, grp, ahead(step)),
                )
            )

    attend_rows(order[-1])
    for ahead_of, step in zip(order[::-1], order[-2::-1]):
        attend_rows(step)
        project_rows(ahead_of)
    project_rows(order[0])

    for load in loads[6:10]:
        load.wait()
    raw = wts[...]
    mixing = (raw / jnp.sum(raw, axis=0, keepdims=True)).astype(jnp.bfloat16).astype(jnp.float32)
    expert = lax.broadcasted_iota(jnp.int32, (LANES, rows_here), 0)
    table = jnp.zeros((LANES, rows_here), jnp.float32)
    for k in range(raw.shape[0]):
        table += jnp.where(ids[k : k + 1, :] == expert, mixing[k : k + 1, :], 0.0)
    unit = (
        lax.broadcasted_iota(jnp.int32, (rows_here, rows_here), 0)
        == lax.broadcasted_iota(jnp.int32, (rows_here, rows_here), 1)
    )
    unit = jnp.where(unit, 1.0, 0.0).astype(jnp.bfloat16)
    table = lax.dot_general(
        unit, table.astype(jnp.bfloat16), NT, preferred_element_type=jnp.float32
    )
    rows[head, side, grp, :, width:] = table.astype(jnp.bfloat16)

    for copy in part_copies:
        copy.wait_recv()
    square = jnp.zeros((rows_here, 1), jnp.float32)
    for piece in range(sides):
        columns = slice(piece * half, (piece + 1) * half)
        value = hid[:, columns].astype(jnp.float32)
        for j in range(heads):
            value += part_in[piece, j].astype(jnp.float32)
        resid[:, columns] = value
        square += jnp.sum(value * value, axis=1, keepdims=True)
    inv_norm = lax.rsqrt(square * (1.0 / width) + 1e-06)
    rows[head, side, grp, :, :width] = (resid[...] * inv_norm * gain[...]).astype(jnp.bfloat16)

    z_copies, sib_copies = [None] * heads, [[] for _ in range(heads)]
    xy_copies = [[None] * groups for _ in range(heads)]
    ys_copies, ya_copies, yb_copies = [None] * heads, [None] * heads, [None] * heads
    zo_copies = []
    own_expert = side * groups + grp
    many = sides * groups * rows_here

    def axes(step):
        return (1, 2) if order.index(step) % 2 == 0 else (2, 1)

    def to_group(step, k, origin):
        piece = rows.at[behind(step), side, group(origin)]
        slot = k if origin == 0 else origin ^ k
        xy_copies[step][slot] = send(
            piece, piece, xy_send.at[step, slot], xy_recv.at[step, slot], (side, group(k), head)
        )

    def to_core(step, origin):
        piece = rows.at[behind(step), side, group(origin)]
        sib_copies[step].append(
            send(
                piece, piece, sib_send.at[step, origin], sib_recv.at[step, origin],
                (other, grp, head),
            )
        )

    def spread(step):
        if step > 0:
            z_copies[step].wait_recv()
        first, second = axes(step)
        to_group(step, first, 0)
        to_group(step, second, 0)
        to_core(step, 0)

    def relay(step):
        first, second = axes(step)
        xy_copies[step][first].wait_recv()
        to_group(step, second, first)
        to_core(step, first)
        xy_copies[step][second].wait_recv()
        to_core(step, second)

    def finish(step):
        xy_copies[step][3].wait_recv()
        to_core(step, 3)

    def experts(step):
        at = behind(step)
        if step == 0:
            for load in loads[10:]:
                load.wait()
        for copy in sib_copies[step]:
            copy.wait_recv()
        x = rows[at, :, :, :, :width].reshape(many, width)
        gate = lax.dot_general(x, wg[...], NT, preferred_element_type=jnp.float32)
        up = lax.dot_general(x, wu[...], NT, preferred_element_type=jnp.float32)
        hidden = (gate / (1.0 + jnp.exp(-gate)) * up).astype(jnp.bfloat16)
        weights = rows[at, :, :, :, width:].reshape(many, LANES).astype(jnp.float32)
        lane = lax.broadcasted_iota(jnp.int32, (many, LANES), 1)
        column = jnp.sum(jnp.where(lane == own_expert, weights, 0.0), axis=1, keepdims=True)
        for n in range(0, width, 2 * CHUNK):
            value = jnp.dot(hidden, wd[:, n : n + 2 * CHUNK], preferred_element_type=jnp.float32)
            value = value.astype(jnp.bfloat16).astype(jnp.float32) * column
            y[at, :, :, :, n : n + 2 * CHUNK] = value.astype(jnp.bfloat16).reshape(
                sides, groups, rows_here, 2 * CHUNK
            )
        ys_copies[step] = send(
            y.at[at, other], y_sib.at[step], ys_send.at[step], ys_recv.at[step],
            (other, grp, head),
        )

    def reduce_cores(step):
        ys_copies[step].wait_recv()
        value = y[behind(step), side].astype(jnp.float32) + y_sib[step].astype(jnp.float32)
        y_sum[step] = value.astype(jnp.bfloat16)
        first, _ = axes(step)
        ya_copies[step] = [
            send(
                y_sum.at[step, group(k)], y_a.at[step, i], ya_send.at[step, i],
                ya_recv.at[step, i], (side, group(first), head),
            )
            for i, k in enumerate((3, first))
        ]

    def reduce_first(step):
        ya_copies[step][0].wait_recv()
        _, second = axes(step)
        value = y_sum[step, group(second)].astype(jnp.float32) + y_a[step, 0].astype(jnp.float32)
        y_fwd[step] = value.astype(jnp.bfloat16)
        yb_copies[step] = send(
            y_fwd.at[step], y_b.at[step], yb_send.at[step], yb_recv.at[step],
            (side, group(second), head),
        )

    def reduce_second(step):
        ya_copies[step][1].wait_recv()
        yb_copies[step].wait_recv()
        value = y_sum[step, grp].astype(jnp.float32) + y_a[step, 1].astype(jnp.float32)
        value += y_b[step].astype(jnp.float32)
        if step == 0:
            resid[...] += value
        else:
            z[step] = value.astype(jnp.bfloat16)
            zo_copies.append(
                send(
                    z.at[step], z_in.at[step], zo_send.at[step], zo_recv.at[step],
                    (side, grp, behind(step)),
                )
            )

    block = rows.at[head, side, grp]
    for step in order[1:]:
        z_copies[step] = send(
            block, block, z_send.at[step], z_recv.at[step], (side, grp, ahead(step))
        )
    stages = (
        (0, spread), (2, relay), (4, finish), (6, experts), (9, reduce_cores),
        (11, reduce_first), (13, reduce_second),
    )
    for _, _, stage, step in sorted(
        (delay + 2 * turn, delay, stage, step)
        for delay, stage in stages
        for turn, step in enumerate(order)
    ):
        stage(step)
    value = resid[...]
    for step, copy in zip(order[1:], zo_copies):
        copy.wait_recv()
        value += z_in[step].astype(jnp.float32)
    out_ref[0] = value.astype(jnp.bfloat16)
    for copy in started:
        copy.wait_send()


def dense_fits(args):
    q_new, hidden_in, expert_ids, w_down = args[0], args[6], args[9], args[13]
    sides, groups, heads = (lax.axis_size(name) for name in ("side", "grp", "head"))
    rows_here, top_k = expert_ids.shape[1:]
    return (
        2 * top_k >= sides * groups
        and sides == 2
        and groups == 4
        and sides * groups <= LANES
        and rows_here % 16 == 0
        and q_new.shape[1] == heads * rows_here
        and args[3].shape[2] % LANES == 0
        and args[7].shape[1] % CHUNK == 0
        and hidden_in.shape[2] % (2 * CHUNK) == 0
    )


def shards_dense(
    q_new, k_cache, value_cache, k_new, new_value_rows, cache_len, hidden_in, out_proj, norm_gain,
    expert_ids, gate_wts, w_gate, w_up, w_down,
):
    sides, groups, heads = (lax.axis_size(name) for name in ("side", "grp", "head"))
    rows_here, width = hidden_in.shape[1:]
    half = out_proj.shape[1]
    operands = (
        q_new, k_cache, value_cache, k_new, new_value_rows, cache_len, hidden_in, out_proj,
        norm_gain.reshape(1, width),
        jnp.swapaxes(expert_ids, 1, 2), jnp.swapaxes(gate_wts, 1, 2),
        jnp.swapaxes(w_gate, 1, 2), jnp.swapaxes(w_up, 1, 2), w_down,
    )
    specs = [pl.BlockSpec(memory_space=pltpu.HBM)] * len(operands)
    specs[5] = pl.BlockSpec(memory_space=pltpu.SMEM)
    bf16 = jnp.bfloat16
    landed = [
        pltpu.VMEM(operands[i].shape[cut:], operands[i].dtype)
        for i, cut in (
            (0, 1), (1, 2), (2, 2), (3, 1), (4, 1), (6, 1), (7, 0), (8, 0), (9, 1), (10, 1),
            (11, 1), (12, 1), (13, 1),
        )
    ]
    dma = pltpu.SemaphoreType.DMA
    return pl.pallas_call(
        dense_kernel,
        out_shape=pltpu.VMEM(hidden_in.shape, bf16),
        in_specs=specs,
        out_specs=pl.BlockSpec(memory_space=pltpu.VMEM),
        scratch_shapes=landed
        + [
            pltpu.VMEM((sides, heads, rows_here, q_new.shape[2]), bf16),
            pltpu.VMEM((sides, heads, rows_here, half), bf16),
            pltpu.VMEM((sides, heads, rows_here, half), bf16),
            pltpu.VMEM((rows_here, width), jnp.float32),
            pltpu.VMEM((heads, sides, groups, rows_here, width + LANES), bf16),
            pltpu.VMEM((heads, sides, groups, rows_here, width), bf16),
            pltpu.VMEM((heads, groups, rows_here, width), bf16),
            pltpu.VMEM((heads, groups, rows_here, width), bf16),
            pltpu.VMEM((heads, 2, rows_here, width), bf16),
            pltpu.VMEM((heads, rows_here, width), bf16),
            pltpu.VMEM((heads, rows_here, width), bf16),
            pltpu.VMEM((heads, rows_here, width), bf16),
            pltpu.VMEM((heads, rows_here, width), bf16),
            dma((len(landed),)),
            dma((heads,)), dma((heads,)),
            dma((sides * heads,)), dma((sides * heads,)),
            dma((heads,)), dma((heads,)),
            dma((heads, groups)), dma((heads, groups)),
            dma((heads, groups)), dma((heads, groups)),
            dma((heads,)), dma((heads,)),
            dma((heads, 2)), dma((heads, 2)),
            dma((heads,)), dma((heads,)),
            dma((heads,)), dma((heads,)),
        ],
        compiler_params=pltpu.CompilerParams(
            collective_id=0, has_side_effects=True, vmem_limit_bytes=60 * 1024 * 1024
        ),
    )(*operands)


def solution(mesh):
    in_specs = (
        P(("side", "grp"), None, "head"),
        P(("side", "grp"), "head", None, None),
        P(("side", "grp"), "head", None, None),
        P(("side", "grp"), None, "head"),
        P(("side", "grp"), None, "head"),
        P(("side", "grp")),
        P(("side", "grp"), "head", None),
        P("head", "side"),
        P(),
        P(("side", "grp"), "head", None),
        P(("side", "grp"), "head", None),
        P(("side", "grp"), None, "head"),
        P(("side", "grp"), None, "head"),
        P(("side", "grp"), "head", None),
    )
    out_specs = P(("side", "grp"), "head", None)
    def shards(*args):
        if dense_fits(args):
            return shards_dense(*args)
        return shards_sparse(*args)

    return jax.shard_map(shards, mesh=mesh, in_specs=in_specs, out_specs=out_specs, check_vma=False)
```
